32 devices in a mesh: groups: 2 (over x), blk: 8 (over z, y), sub: 2 (over core).
Axes of the slice: x: 2, y: 2, z: 4, core: 2. Of those that a mesh axis runs over, the one named last changes fastest.
Arguments:
- queries: bfloat16 [128, 32, 128], P(('groups', 'blk', 'sub')), parts along dimension 0, may hold values from -0.59765625 to 0.59765625
- candidates: int32 [128, 128], P(('groups', 'blk', 'sub')), parts along dimension 0, may hold values from 0 to 255, all different within a row; in each aligned block of 64 rows (0 to 63, 64 to 127, ...) at most 48 rows name the same one
- location: int32 [256], replicated, may hold values from 0 to 255, each once
- lengths: int32 [256], P(('blk', 'sub')), may hold values from 32 to 128
- centroid_ids: int32 [32768], P(('blk', 'sub')), may hold values from 0 to 262143, as said below
- residual_codes: int32 [32768, 128], P(('blk', 'sub')), may hold values from 0 to 3
- centroids: bfloat16 [262144, 128], P('blk'), may hold values from -0.5 to 0.5
- buckets: float32 [4, 128], replicated, may hold values from -0.4 to 0.4
Outputs:
- maxsim_scores: float32 [128, 128], P(('groups', 'blk', 'sub')), parts along dimension 0
The draws below stay inside these ranges and needn't reach their ends.
There are 2 independent parts, one for each index of `groups`. The reference program is written for one: setup_inputs(seed, part) draws one part's arguments, and reference() takes and returns one part's arrays. A program takes and returns all parts, laid end to end along the dimension named above; an argument that names none is the same for every part. Nothing has to cross between parts.
Inputs may be any that keep to these rules, and one draw needn't show every extreme that they name: `candidates`: each query names 128 distinct passages; no passage is named by more than 48 queries, a bound that some block reaches. `location`: a permutation; slots s * 16 to (s + 1) * 16 - 1 are those of the s-th device along blk+sub. `centroid_ids`: among the 2048 token rows of one device, at most 512 have centroids in any one block of 32768 consecutive ids, and exactly 512 in some block, on every device.
All inputs are finite; a program needn't handle non-finite values.
Results may differ from the reference program's by a relative error of at most 0.0003.
Values may be sent and summed in bfloat16 or wider, within the bound.
No kernel may reach another device: no remote copies, remote signals or barrier semaphores. Data moves between devices by JAX's collectives and lax.ppermute only.
A program may use at most 64 MiB of HBM per device.

```python
import math
import jax
import jax.numpy as jnp
import numpy as np
from jax import lax

D = 128
C = 262144
QT = 32
L = 128
NBUCKET = 4
K = 128
OWNERS = 16
NPASS = 256
Q = 64
CSHARD = 32768
TOKD = 2048
QCAP = 48


def draw_centroid_ids(key, part):
    key = jax.random.fold_in(key, 11)
    shard_total = C // CSHARD
    mean_load = TOKD // shard_total
    pair_count = shard_total // 2

    def device_block(block_key):
        subkeys = jax.random.split(block_key, 5)
        spread = jax.random.randint(subkeys[0], (pair_count,), -(mean_load // 2), mean_load // 2 + 1)
        hot_pair = jax.random.randint(subkeys[1], (), 0, pair_count)
        first_load = jnp.where(jnp.arange(pair_count) == hot_pair, 2 * mean_load, mean_load + spread)
        second_load = 2 * mean_load - first_load
        flipped = jax.random.randint(subkeys[2], (pair_count,), 0, 2)
        upper_load = jnp.where(flipped == 1, second_load, first_load)
        lower_load = jnp.where(flipped == 1, first_load, second_load)
        loads = jnp.stack([upper_load, lower_load], axis=1).reshape(shard_total)
        load_ends = jnp.cumsum(loads)
        positions = jnp.arange(TOKD)
        shard_of = jnp.sum((positions[:, None] >= load_ends[None, :]).astype(jnp.int32), axis=1)
        shard_of = jax.random.permutation(subkeys[3], shard_of)
        offsets = jax.random.randint(subkeys[4], (TOKD,), 0, CSHARD)
        return shard_of * CSHARD + offsets
    block_keys = jax.random.split(key, OWNERS)
    return jax.vmap(device_block)(block_keys).reshape(OWNERS * TOKD).astype(jnp.int32)


def with_ends(values, own_key, smallest, largest):
    longest = values.shape.index(max(values.shape))
    spots = []
    for shift in (0, 1):
        where = [jax.random.randint(jax.random.fold_in(own_key, axis), (), 0, length) for axis, length in enumerate(values.shape)]
        where[longest] = (where[longest] + shift) % values.shape[longest]
        spots.append(tuple(where))
    return values.at[spots[0]].set(smallest).at[spots[1]].set(largest)


def shard_levels(own_key, dims, pieces, smallest, largest):
    level, own = 1.0, jax.random.fold_in(own_key, 6)
    for position, shards_of in pieces:
        steps = jnp.exp(jax.random.uniform(jax.random.fold_in(own, position), (shards_of,), jnp.float32, smallest / len(pieces), largest / len(pieces)))
        level = level * jnp.repeat(steps, dims[position] // shards_of).reshape([-1 if axis == position else 1 for axis in range(len(dims))])
    return level


def routed_block(stream_key, own, number, rows, count, top, limit, skew):
    sequence = jax.random.permutation(stream_key, count)
    packed, ordinary = load_shares(count, rows * top, limit, skew, True), load_shares(count, rows * top, limit, skew, False)
    places = jnp.arange(count)

    def named(sizes, rotation):
        used = int((sizes > 0).sum())
        fixed = max(1, used // 4)
        passed = fixed + (places - fixed + rotation * (used - fixed)) % max(1, count - fixed)
        return jnp.zeros((count,), jnp.int32).at[sequence[jnp.where(places < fixed, places, passed)]].set(jnp.asarray(sizes, jnp.int32))

    sizes = jnp.where(number % 4 == 0, named(packed, number // 4), named(ordinary, number - number // 4 - 1))
    mixed = jax.random.permutation(jax.random.fold_in(own, 3), count)
    giver, receiver = mixed[0:count // 2 * 2:2], mixed[1:count // 2 * 2:2]
    slack = jnp.minimum(sizes[giver] - 1, limit - sizes[receiver]) // 2
    slack = jnp.where((giver == sequence[0]) | (receiver == sequence[0]) | (sizes[receiver] == 0), 0, jnp.maximum(slack, 0))
    passed = jax.random.randint(jax.random.fold_in(own, 4), (count // 2,), 0, 1 << 20) % (slack + 1)
    sizes = sizes.at[giver].add(-passed).at[receiver].add(passed)
    members = jnp.searchsorted(jnp.cumsum(sizes), jnp.arange(rows * top), side="right").astype(jnp.int32)
    grid = members.reshape(top, rows).T
    grid = grid[jax.random.permutation(jax.random.fold_in(own, 1), rows)]
    rotation = jax.random.randint(jax.random.fold_in(own, 2), (rows, 1), 0, top)
    return jnp.take_along_axis(grid, (jnp.arange(top)[None, :] + rotation) % top, axis=1)


def load_shares(amount, total, reach, lean, full):
    weights = [(1 << 20) // math.isqrt(standing ** lean) + 1 for standing in range(1, amount + 1)]
    largest = reach if full else min(reach, max(-(-total // amount), total * weights[0] // sum(weights)))
    least = 1 if total - largest >= amount - 1 else 0
    given, surplus = [largest] + [least] * (amount - 1), total - largest - least * (amount - 1)
    while surplus > 0:
        free = [i for i in range(1, amount) if given[i] < largest] or [i for i in range(1, amount) if given[i] < reach]
        whole, remaining = sum([weights[i] for i in free]), surplus
        for i in free:
            extra = min(reach - given[i], max(1, remaining * weights[i] // whole), surplus)
            given[i] = given[i] + extra
            surplus = surplus - extra
    return np.array(given)


def centred(rng, shape, width, most, cuts=(), held_as=jnp.bfloat16):
    array = jax.random.normal(rng, shape, jnp.float32) * width
    if len(cuts) > 0:
        array = shard_levels(rng, shape, cuts, -0.22, 0.18) * array
    return jnp.clip(array, min=-most, max=most).astype(held_as)


def setup_inputs(seed: int = 0, part: int = 0) -> dict:
    seeds = jax.random.split(jax.random.key(seed), 9)
    own_keys = jax.random.split(jax.random.fold_in(seeds[8], part), 9)
    queries = centred(own_keys[0], (Q, QT, D), 0.09, 0.59765625, ((0, 16),))
    candidates_keys = jax.random.split(jax.random.fold_in(own_keys[1], 1), Q // Q)
    candidates_turns = jax.random.permutation(jax.random.fold_in(own_keys[1], 3), Q // Q)
    candidates = jax.vmap(lambda own, number: routed_block(jax.random.fold_in(own_keys[1], 2), own, number, Q, NPASS, K, QCAP, 2))(candidates_keys, candidates_turns).reshape((Q, K))
    location = jax.random.permutation(seeds[2], NPASS).astype(jnp.int32)
    lengths = with_ends(jax.random.randint(seeds[3], (NPASS,), L // 4, L + 1), jax.random.fold_in(seeds[3], 1), L // 4, L).astype(jnp.int32)
    centroid_ids = draw_centroid_ids(jax.random.fold_in(seeds[8], 71), part)
    residual_codes = with_ends(jax.random.randint(seeds[5], (NPASS * L, D), 0, NBUCKET), jax.random.fold_in(seeds[5], 1), 0, NBUCKET - 1).astype(jnp.int32)
    centroids = centred(seeds[6], (C, D), D ** -0.5, 0.5, ((0, 8),))
    buckets = centred(seeds[7], (NBUCKET, D), 0.08, 0.4, (), jnp.float32)
    return dict(queries=queries, candidates=candidates, location=location, lengths=lengths, centroid_ids=centroid_ids, residual_codes=residual_codes, centroids=centroids, buckets=buckets)


def decompress(centroid_ids, residual_codes, centroids, buckets):
    residual = jnp.where(residual_codes == 0, buckets[0], jnp.where(residual_codes == 1, buckets[1], jnp.where(residual_codes == 2, buckets[2], buckets[3])))
    centroid_rows = jnp.take(centroids, centroid_ids, axis=0).astype(jnp.float32)
    return (centroid_rows + residual).astype(jnp.bfloat16)


def reference(queries, candidates, location, lengths, centroid_ids, residual_codes, centroids, buckets):
    embedded = decompress(centroid_ids, residual_codes, centroids, buckets).reshape(NPASS, L, D)
    slots = jnp.take(location, candidates, axis=0).astype(jnp.int32)
    positions = jnp.arange(L, dtype=jnp.int32)

    def one_query(query_row):
        query_matrix = queries[query_row].astype(jnp.float32)
        slot_row = slots[query_row]
        chosen = jnp.take(embedded, slot_row, axis=0).astype(jnp.float32)
        live_rows = positions[None, :] < jnp.take(lengths, slot_row)[:, None]
        scores = jnp.einsum("td,kjd->ktj", query_matrix, chosen)
        scores = jnp.where(live_rows[:, None, :], scores, -1e30)
        return jnp.sum(jnp.max(scores, axis=2), axis=1)

    return lax.map(one_query, jnp.arange(Q, dtype=jnp.int32))
```

```python
import functools

import jax
import jax.numpy as jnp
from jax import lax
from jax.experimental import pallas as pl
from jax.experimental.pallas import tpu as pltpu
from jax.sharding import PartitionSpec as P

F32 = jnp.float32
BF16 = jnp.bfloat16
I32 = jnp.int32
MIB = 1 << 20


def dot_nt(a, b):
    return lax.dot_general(a, b, (((1,), (1,)), ((), ())), preferred_element_type=F32)


def dot_nn(a, b):
    return lax.dot_general(a, b, (((1,), (0,)), ((), ())), preferred_element_type=F32)


def plan_kernel(shards, shard_rows, cap, lengths_ref, ids_ref, requests_ref, pos_ref):
    passages, height = ids_ref.shape
    ids = ids_ref[...]
    owner = ids // shard_rows
    offset = ids - owner * shard_rows
    row = lax.broadcasted_iota(I32, (passages, height), 0)
    lane = lax.broadcasted_iota(I32, (passages, height), 1)
    limit = jnp.zeros((passages, height), I32)
    for p in range(passages):
        limit = jnp.where(row == p, lengths_ref[p], limit)
    owner = jnp.where(lane < limit, owner, shards)
    mask = jnp.concatenate([jnp.where(owner == b, 1.0, 0.0) for b in range(shards)], axis=0)
    mask16 = mask.astype(BF16)
    k = lax.broadcasted_iota(I32, (height, height), 0)
    l = lax.broadcasted_iota(I32, (height, height), 1)
    inside = dot_nn(mask16, jnp.where(k < l, 1.0, 0.0).astype(BF16))
    totals = dot_nn(mask16, jnp.ones((height, height), BF16))
    full = shards * passages
    r = lax.broadcasted_iota(I32, (full, full), 0)
    c = lax.broadcasted_iota(I32, (full, full), 1)
    same = r // passages == c // passages
    totals16 = totals.astype(BF16)
    ahead = dot_nn(jnp.where(same & (c < r), 1.0, 0.0).astype(BF16), totals16)
    place = (inside + ahead) * mask
    rank = jnp.zeros((passages, height), F32)
    counts = []
    for b in range(shards):
        rank = rank + place[b * passages : (b + 1) * passages]
        counts.append(jnp.sum(totals[b * passages : (b + 1) * passages], axis=0, keepdims=True))
    pos = owner * cap + rank.astype(I32)
    pos_ref[...] = jnp.where(lane < limit, pos, 0)
    pos_row = pos // height
    pos_lane = pos - pos_row * height
    high = (offset // 256).astype(F32)
    low = (offset % 256).astype(F32)
    rows = shards * cap // height
    out_row = lax.broadcasted_iota(I32, (rows, height), 0)
    out_lane = lax.broadcasted_iota(I32, (height, height), 0)
    total = jnp.zeros((rows, 2 * height), F32)
    for p in range(passages):
        here = jnp.where(out_row == pos_row[p : p + 1], 1.0, 0.0).astype(BF16)
        hit = out_lane == pos_lane[p : p + 1]
        values = jnp.concatenate(
            [jnp.where(hit, high[p : p + 1], 0.0), jnp.where(hit, low[p : p + 1], 0.0)], axis=0
        ).astype(BF16)
        total = total + dot_nt(here, values)
    found = (total[:, :height] * 256.0 + total[:, height:]).astype(I32)
    per = rows // shards
    for b in range(shards):
        requests_ref[b * per : (b + 1) * per] = (
            found[b * per : (b + 1) * per] + counts[b].astype(I32) * shard_rows
        )


def plan(lengths, ids, shards, shard_rows, cap):
    passages, height = ids.shape
    return pl.pallas_call(
        functools.partial(plan_kernel, shards, shard_rows, cap),
        out_shape=(
            jax.ShapeDtypeStruct((shards * cap // height, height), I32),
            jax.ShapeDtypeStruct((passages, height), I32),
        ),
        in_specs=[
            pl.BlockSpec(memory_space=pltpu.SMEM),
            pl.BlockSpec(memory_space=pltpu.VMEM),
        ],
        out_specs=(
            pl.BlockSpec(memory_space=pltpu.VMEM),
            pl.BlockSpec(memory_space=pltpu.VMEM),
        ),
        compiler_params=pltpu.CompilerParams(vmem_limit_bytes=16 * MIB),
    )(lengths, ids)


def widen_kernel(chunk, source_ref, wide_ref, buffers, sems):
    steps = source_ref.shape[0] // chunk

    def copy(step, slot):
        return pltpu.make_async_copy(
            source_ref.at[pl.ds(step * chunk, chunk)], buffers.at[slot], sems.at[slot]
        )

    copy(0, 0).start()
    for step in range(steps):
        if step + 1 < steps:
            copy(step + 1, (step + 1) % 2).start()
        copy(step, step % 2).wait()

        @pl.loop(0, chunk // 256)
        def _(i):
            at = pl.multiple_of(i * 256, 256)
            wide_ref[pl.ds(step * chunk + at, 256)] = buffers[step % 2, pl.ds(at, 256)].astype(F32)


def widen(centroids):
    rows, width = centroids.shape
    chunk = min(rows, 4096)
    return pl.pallas_call(
        functools.partial(widen_kernel, chunk),
        out_shape=jax.ShapeDtypeStruct((rows, width), F32),
        in_specs=[pl.BlockSpec(memory_space=pl.ANY)],
        out_specs=pl.BlockSpec(memory_space=pltpu.VMEM),
        scratch_shapes=[pltpu.VMEM((2, chunk, width), BF16), pltpu.SemaphoreType.DMA((2,))],
        compiler_params=pltpu.CompilerParams(vmem_limit_bytes=40 * MIB),
    )(centroids)


UNROLL = 16


def fetch_kernel(shards, shard_rows, cap, asked_ref, table_ref, out_ref, wide):
    @pl.loop(0, shards)
    def _(d):
        base = d * cap
        count = asked_ref[base] // shard_rows

        @pl.loop(0, (count + UNROLL - 1) // UNROLL)
        def _(i):
            at = pl.multiple_of(base + i * UNROLL, UNROLL)
            for u in range(UNROLL):
                offset = lax.rem(asked_ref[at + u], shard_rows)
                wide[pl.ds(at + u, 1)] = table_ref[pl.ds(offset, 1)]

    @pl.loop(0, shards * cap // 256)
    def _(i):
        at = pl.multiple_of(i * 256, 256)
        out_ref[pl.ds(at, 256)] = wide[pl.ds(at, 256)].astype(BF16)


def fetch(asked, table, shards, shard_rows, cap):
    width = table.shape[1]
    return pl.pallas_call(
        functools.partial(fetch_kernel, shards, shard_rows, cap),
        out_shape=jax.ShapeDtypeStruct((shards * cap, width), BF16),
        in_specs=[
            pl.BlockSpec(memory_space=pltpu.SMEM),
            pl.BlockSpec(memory_space=pltpu.VMEM),
        ],
        out_specs=pl.BlockSpec(memory_space=pltpu.VMEM),
        scratch_shapes=[pltpu.VMEM((shards * cap, width), F32)],
        compiler_params=pltpu.CompilerParams(vmem_limit_bytes=40 * MIB),
    )(asked, table)


def score_kernel(
    span, lengths_ref, pos_ref, replies_ref, codes_ref, buckets_ref, queries_ref, out_ref, wide, tile
):
    passages, height = codes_ref.shape[0], codes_ref.shape[1]
    width = codes_ref.shape[2]
    owners = queries_ref.shape[0] // span
    chunk = 2 * span

    @pl.loop(0, replies_ref.shape[0] // 256)
    def _(i):
        at = pl.multiple_of(i * 256, 256)
        wide[pl.ds(at, 256)] = replies_ref[pl.ds(at, 256)].astype(F32)

    levels = [jnp.broadcast_to(buckets_ref[b : b + 1], (height, width)) for b in range(4)]
    line = lax.broadcasted_iota(I32, (height, width), 0)

    @pl.loop(0, passages)
    def _(p):
        length = lengths_ref[p]

        @pl.loop(0, (length + UNROLL - 1) // UNROLL)
        def _(i):
            at = pl.multiple_of(i * UNROLL, UNROLL)
            for u in range(UNROLL):
                tile[pl.ds(at + u, 1)] = wide[pl.ds(pos_ref[p * height + at + u], 1)]

        codes = codes_ref[p]
        residual = jnp.where(
            codes == 0,
            levels[0],
            jnp.where(codes == 1, levels[1], jnp.where(codes == 2, levels[2], levels[3])),
        )
        rows = tile[...] + residual
        rows = jnp.where(line < length, rows, rows[0:1])
        embedded = rows.astype(BF16)
        for c in range(owners // 2):
            scores = dot_nt(embedded, queries_ref[c * chunk : (c + 1) * chunk])
            best = jnp.max(scores, axis=0, keepdims=True)
            out_ref[2 * c, pl.ds(p, 1)] = best[:, :span]
            out_ref[2 * c + 1, pl.ds(p, 1)] = best[:, span:]


def score(lengths, pos, replies, codes, buckets, queries, span):
    passages, height, width = codes.shape
    owners = queries.shape[0] // span
    return pl.pallas_call(
        functools.partial(score_kernel, span),
        out_shape=jax.ShapeDtypeStruct((owners, passages, span), F32),
        in_specs=[
            pl.BlockSpec(memory_space=pltpu.SMEM),
            pl.BlockSpec(memory_space=pltpu.SMEM),
            pl.BlockSpec(memory_space=pltpu.VMEM),
            pl.BlockSpec(memory_space=pltpu.VMEM),
            pl.BlockSpec(memory_space=pltpu.VMEM),
            pl.BlockSpec(memory_space=pltpu.VMEM),
        ],
        out_specs=pl.BlockSpec(memory_space=pltpu.VMEM),
        scratch_shapes=[
            pltpu.VMEM((replies.shape[0], width), F32),
            pltpu.VMEM((height, width), F32),
        ],
        compiler_params=pltpu.CompilerParams(vmem_limit_bytes=40 * MIB),
    )(lengths, pos, replies, codes, buckets, queries)


def pick_kernel(tokens, location_ref, candidates_ref, best_ref, out_ref):
    owned, listed = candidates_ref.shape
    slots_total, span = best_ref.shape
    groups, width = location_ref.shape
    which = lax.broadcasted_iota(I32, (width, listed), 0)
    slot = lax.broadcasted_iota(I32, (slots_total, listed), 0)
    sums = best_ref[...]
    shift = tokens // 2
    while shift:
        sums = sums + pltpu.roll(sums, span - shift, 1)
        shift //= 2
    for q in range(owned):
        named = candidates_ref[q : q + 1]
        found = jnp.zeros((2, listed), F32)
        for g in range(groups):
            here = location_ref[g : g + 1]
            pair = jnp.concatenate([here // 256, here % 256], axis=0).astype(F32).astype(BF16)
            hit = jnp.where(which + g * width == named, 1.0, 0.0).astype(BF16)
            found = found + dot_nn(pair, hit)
        slots = (found[0:1] * 256.0 + found[1:2]).astype(I32)
        column = jnp.broadcast_to(sums[:, q * tokens : q * tokens + 1], (slots_total, listed))
        out_ref[q : q + 1] = jnp.sum(jnp.where(slot == slots, column, 0.0), axis=0, keepdims=True)


def pick(location, candidates, best, tokens):
    return pl.pallas_call(
        functools.partial(pick_kernel, tokens),
        out_shape=jax.ShapeDtypeStruct(candidates.shape, F32),
        compiler_params=pltpu.CompilerParams(vmem_limit_bytes=16 * MIB),
    )(location, candidates, best)


def body(queries, candidates, location, lengths, centroid_ids, residual_codes, centroids, buckets):
    token_count = centroid_ids.shape[0]
    passage_count = lengths.shape[0]
    height = token_count // passage_count
    width = residual_codes.shape[1]
    shard_rows = centroids.shape[0]
    shards = lax.axis_size("blk")
    owners = shards * lax.axis_size("sub")
    cap = 2 * token_count // shards
    owned, tokens = queries.shape[0], queries.shape[1]
    span = owned * tokens

    requests, pos = plan(
        lengths, centroid_ids.reshape(passage_count, height), shards, shard_rows, cap
    )
    asked = lax.all_to_all(
        requests.reshape(shards, cap), "blk", split_axis=0, concat_axis=0, tiled=True
    )
    table = widen(centroids)
    sent = jnp.broadcast_to(queries.reshape(1, span, width), (owners, span, width))
    all_queries = lax.all_to_all(sent, ("blk", "sub"), split_axis=0, concat_axis=0, tiled=True)
    found = fetch(asked.reshape(shards * cap), table, shards, shard_rows, cap)
    replies = lax.all_to_all(
        found.reshape(shards, cap, width), "blk", split_axis=0, concat_axis=0, tiled=True
    )
    best = score(
        lengths,
        pos.reshape(token_count),
        replies.reshape(shards * cap, width),
        residual_codes.reshape(passage_count, height, width),
        buckets,
        all_queries.reshape(owners * span, width),
        span,
    )
    mine = lax.all_to_all(best, ("blk", "sub"), split_axis=0, concat_axis=0, tiled=True)
    return pick(
        location.reshape(location.shape[0] // 128, 128),
        candidates,
        mine.reshape(owners * passage_count, span),
        tokens,
    )


def solution(mesh):
    in_specs = (
        P(("groups", "blk", "sub"), None, None),
        P(("groups", "blk", "sub"), None),
        P(),
        P(("blk", "sub")),
        P(("blk", "sub")),
        P(("blk", "sub"), None),
        P("blk", None),
        P(),
    )
    out_specs = P(("groups", "blk", "sub"), None)
    return jax.shard_map(body, mesh=mesh, in_specs=in_specs, out_specs=out_specs, check_vma=False)
```

```python
import functools

import jax
import jax.numpy as jnp
from jax import lax
from jax.experimental import pallas as pl
from jax.experimental.pallas import tpu as pltpu
from jax.sharding import PartitionSpec as P

F32 = jnp.float32
BF16 = jnp.bfloat16
I32 = jnp.int32
MIB = 1 << 20
UNROLL = 16
TILE = 16
COUNT_AT = 1 << 18
SMEM = pl.BlockSpec(memory_space=pltpu.SMEM)
VMEM = pl.BlockSpec(memory_space=pltpu.VMEM)
HBM = pl.BlockSpec(memory_space=pl.ANY)


def dot_nt(a, b):
    return lax.dot_general(a, b, (((1,), (1,)), ((), ())), preferred_element_type=F32)


def dot_nn(a, b):
    return lax.dot_general(a, b, (((1,), (0,)), ((), ())), preferred_element_type=F32)


def plan_kernel(
    shards, shard_rows, cap, parts, lengths_hbm, ids_hbm, queries_hbm, sent_ref, pos_ref,
    lengths_ref, ids_ref, queries_ref, sems,
):
    copies = [
        pltpu.make_async_copy(lengths_hbm, lengths_ref, sems.at[0]),
        pltpu.make_async_copy(ids_hbm, ids_ref, sems.at[1]),
        pltpu.make_async_copy(queries_hbm, queries_ref, sems.at[2]),
    ]
    for copy in copies:
        copy.start()
    for copy in copies:
        copy.wait()
    passages, height = ids_ref.shape
    span = queries_ref.shape[0]
    part = lax.axis_index("groups")
    ids = ids_ref[...]
    owner = ids // shard_rows
    offset = ids - owner * shard_rows
    row = lax.broadcasted_iota(I32, (passages, height), 0)
    lane = lax.broadcasted_iota(I32, (passages, height), 1)
    limit = jnp.zeros((passages, height), I32)
    for p in range(passages):
        limit = jnp.where(row == p, lengths_ref[p], limit)
    owner = jnp.where(lane < limit, owner, shards)
    mask = jnp.concatenate([jnp.where(owner == b, 1.0, 0.0) for b in range(shards)], axis=0)
    mask16 = mask.astype(BF16)
    k = lax.broadcasted_iota(I32, (height, height), 0)
    l = lax.broadcasted_iota(I32, (height, height), 1)
    inside = dot_nn(mask16, jnp.where(k < l, 1.0, 0.0).astype(BF16))
    totals = dot_nn(mask16, jnp.ones((height, height), BF16))
    full = shards * passages
    r = lax.broadcasted_iota(I32, (full, full), 0)
    c = lax.broadcasted_iota(I32, (full, full), 1)
    same = r // passages == c // passages
    ahead = dot_nn(jnp.where(same & (c < r), 1.0, 0.0).astype(BF16), totals.astype(BF16))
    place = (inside + ahead) * mask
    rank = jnp.zeros((passages, height), F32)
    for b in range(shards):
        rank = rank + place[b * passages : (b + 1) * passages]
    rank = rank.astype(I32)
    mine = (lane < limit) & (rank % parts == part)
    rank = rank // parts
    pos_ref[...] = jnp.where(mine, owner * cap + rank, -1)
    per = list_rows(cap, height)
    list_row = jnp.where(mine, owner * per + rank // height, -1)
    list_lane = rank % height
    high = (offset // 256).astype(F32)
    low = (offset % 256).astype(F32)
    rows = shards * per
    out_row = lax.broadcasted_iota(I32, (rows, height), 0)
    at_lane = lax.broadcasted_iota(I32, (height, height), 0)
    sums = jnp.zeros((rows, 2 * height), F32)
    for p in range(passages):
        here = jnp.where(out_row == list_row[p : p + 1], 1.0, 0.0).astype(BF16)
        hit = at_lane == list_lane[p : p + 1]
        values = jnp.concatenate(
            [jnp.where(hit, high[p : p + 1], 0.0), jnp.where(hit, low[p : p + 1], 0.0)], axis=0
        ).astype(BF16)
        sums = sums + dot_nt(here, values)
    queries = queries_ref[...]
    extra = message_rows(cap, height)
    for b in range(shards):
        total = jnp.sum(totals[b * passages : (b + 1) * passages], axis=0, keepdims=True)
        share = (total.astype(I32) + (parts - 1 - part)) // parts
        sent_ref[b, :span] = queries
        sent_ref[b, span:] = jnp.concatenate(
            [
                sums[b * per : (b + 1) * per, :height],
                sums[b * per : (b + 1) * per, height:],
                share.astype(F32),
                jnp.zeros((extra - 2 * per - 1, height), F32),
            ],
            axis=0,
        ).astype(BF16)


def list_rows(cap, lanes):
    return (cap + lanes - 1) // lanes


def message_rows(cap, lanes):
    return (2 * list_rows(cap, lanes) + TILE) // TILE * TILE


def plan(lengths, ids, queries, shards, shard_rows, cap, parts):
    passages, height = ids.shape
    span = queries.shape[0]
    return pl.pallas_call(
        functools.partial(plan_kernel, shards, shard_rows, cap, parts),
        out_shape=(
            jax.ShapeDtypeStruct((shards, span + message_rows(cap, height), height), BF16),
            jax.ShapeDtypeStruct((passages, height), I32),
        ),
        in_specs=[HBM, HBM, HBM],
        out_specs=(VMEM, VMEM),
        scratch_shapes=[
            pltpu.SMEM(lengths.shape, I32),
            pltpu.VMEM(ids.shape, I32),
            pltpu.VMEM(queries.shape, BF16),
            pltpu.SemaphoreType.DMA((3,)),
        ],
        compiler_params=pltpu.CompilerParams(vmem_limit_bytes=8 * MIB),
    )(lengths, ids, queries)


def order_kernel(pos_ref, list_ref):
    passages, height = pos_ref.shape
    pos = pos_ref[...]
    mine = jnp.where(pos >= 0, 1.0, 0.0).astype(BF16)
    k = lax.broadcasted_iota(I32, (height, height), 0)
    l = lax.broadcasted_iota(I32, (height, height), 1)
    rank = dot_nn(mine, jnp.where(k < l, 1.0, 0.0).astype(BF16))
    total = dot_nn(mine, jnp.ones((height, height), BF16))
    rank = jnp.where(pos >= 0, rank.astype(I32), -1)
    high = (pos // 256).astype(F32)
    low = (pos % 256).astype(F32)
    token = lax.broadcasted_iota(I32, (1, height), 1).astype(F32)
    for p in range(passages):
        hit = jnp.where(k == rank[p : p + 1], 1.0, 0.0).astype(BF16)
        values = jnp.concatenate([high[p : p + 1], low[p : p + 1], token], axis=0).astype(BF16)
        found = dot_nt(values, hit)
        place = found[0:1] * 256.0 + found[1:2]
        entry = (place * height + found[2:3]).astype(I32)
        list_ref[p : p + 1] = entry + total[p : p + 1].astype(I32) * COUNT_AT


def order(pos):
    return pl.pallas_call(
        order_kernel,
        out_shape=jax.ShapeDtypeStruct(pos.shape, I32),
        in_specs=[VMEM],
        out_specs=VMEM,
        compiler_params=pltpu.CompilerParams(vmem_limit_bytes=8 * MIB),
    )(pos)


def fetch_kernel(span, cap, received_ref, table_ref, out_ref, ask, asked, sem):
    shards = received_ref.shape[0]
    height = received_ref.shape[2]
    width = table_ref.shape[1]
    per = list_rows(cap, height)
    for d in range(shards):
        message = received_ref[d, span:].astype(F32)
        ask[d, :per] = (message[:per] * 256.0 + message[per : 2 * per]).astype(I32)
        ask[d, per : per + 1] = message[2 * per : 2 * per + 1].astype(I32)
    copy = pltpu.make_async_copy(ask, asked, sem)
    copy.start()
    copy.wait()
    line = lax.broadcasted_iota(I32, (8, width), 0)

    @pl.loop(0, shards)
    def _(d):
        count = asked[d, per, 0]

        @pl.loop(0, (count + TILE - 1) // TILE)
        def _(i):
            halves = [jnp.zeros((8, width), F32), jnp.zeros((8, width), F32)]
            at = i * TILE
            at_row, at_lane = at // height, lax.rem(at, height)
            for u in range(TILE):
                offset = asked[d, at_row, at_lane + u]
                low = offset & (TILE - 1)
                near = pl.multiple_of(offset - low, TILE)
                rows = table_ref[pl.ds(near, TILE)].astype(F32)
                row = jnp.where(low >= 8, rows[8:], rows[:8])
                row = pltpu.roll(row, (u - low) & 7, 0)
                halves[u // 8] = jnp.where(line == u % 8, row, halves[u // 8])
            to = pl.multiple_of(d * cap + at, TILE)
            out_ref[pl.ds(to, TILE)] = jnp.concatenate(halves, axis=0).astype(BF16)


def fetch(received, table, span, cap):
    width = table.shape[1]
    shards, _, height = received.shape
    ask_rows = (list_rows(cap, height) + 8) // 8 * 8
    return pl.pallas_call(
        functools.partial(fetch_kernel, span, cap),
        out_shape=jax.ShapeDtypeStruct((shards * cap, width), BF16),
        in_specs=[VMEM, VMEM],
        out_specs=VMEM,
        scratch_shapes=[
            pltpu.VMEM((shards, ask_rows, height), I32),
            pltpu.SMEM((shards, ask_rows, height), I32),
            pltpu.SemaphoreType.DMA,
        ],
        compiler_params=pltpu.CompilerParams(vmem_limit_bytes=24 * MIB),
    )(received, table)


def block_rows(height, shards, parts):
    most = min(height, (height + shards * (parts - 1)) // parts)
    return (most + 7) // 8 * 8


def residual_kernel(list_ref, codes_ref, buckets_ref, out_ref, picked):
    passages, block, width = out_ref.shape
    height = codes_ref.shape[1]

    @pl.loop(0, passages)
    def _(p):
        count = list_ref[p * height] // COUNT_AT

        @pl.loop(0, (count + UNROLL - 1) // UNROLL)
        def _(i):
            at = pl.multiple_of(i * UNROLL, UNROLL)
            for u in range(UNROLL):
                token = list_ref[p * height + at + u] & (height - 1)
                picked[pl.ds(at + u, 1)] = codes_ref[p, pl.ds(token, 1)]

        codes = picked[:block]
        out_ref[p] = jnp.where(
            codes == 0,
            buckets_ref[0:1],
            jnp.where(
                codes == 1,
                buckets_ref[1:2],
                jnp.where(codes == 2, buckets_ref[2:3], buckets_ref[3:4]),
            ),
        )


def residual(lists, codes, buckets, block):
    passages, height, width = codes.shape
    return pl.pallas_call(
        residual_kernel,
        out_shape=jax.ShapeDtypeStruct((passages, block, width), F32),
        in_specs=[SMEM, VMEM, VMEM],
        out_specs=VMEM,
        scratch_shapes=[pltpu.VMEM((block + UNROLL, width), I32)],
        compiler_params=pltpu.CompilerParams(vmem_limit_bytes=16 * MIB),
    )(lists, codes, buckets)


def score_kernel(span, list_ref, replies_ref, residual_ref, *refs):
    passages, block, width = residual_ref.shape
    *query_refs, out_ref, wide, tile, embedded = refs
    groups, subs = lax.axis_size("groups"), lax.axis_size("sub")
    own_group, own_sub = lax.axis_index("groups"), lax.axis_index("sub")
    shards = query_refs[0].shape[0]
    height = list_ref.shape[0] // passages
    pair = 2 if shards % 2 == 0 else 1

    @pl.loop(0, replies_ref.shape[0] // 256)
    def _(i):
        at = pl.multiple_of(i * 256, 256)
        wide[pl.ds(at, 256)] = replies_ref[pl.ds(at, 256)].astype(F32)

    @pl.loop(0, passages)
    def _(p):
        count = list_ref[p * height] // COUNT_AT

        @pl.loop(0, (count + UNROLL - 1) // UNROLL)
        def _(i):
            at = pl.multiple_of(i * UNROLL, UNROLL)
            for u in range(UNROLL):
                place = (list_ref[p * height + at + u] & (COUNT_AT - 1)) // height
                tile[pl.ds(p * block + at + u, 1)] = wide[pl.ds(place, 1)]

    line = lax.broadcasted_iota(I32, (block, width), 0)
    here = lax.broadcasted_iota(I32, (passages, pair * span), 0)
    counts = jnp.zeros((passages, pair * span), I32)
    for p in range(0, passages, 2):
        both = []
        for q in (p, p + 1):
            count = list_ref[q * height] // COUNT_AT
            counts = jnp.where(here == q, count, counts)
            rows = tile[q * block : (q + 1) * block] + residual_ref[q]
            both.append(jnp.where(line < count, rows, rows[0:1]))
        embedded[p * block : (p + 2) * block] = jnp.concatenate(both, axis=0).astype(BF16)

    for step, query_ref in enumerate(query_refs):
        group = lax.rem(own_group + groups - step // subs, groups)
        sub = lax.rem(own_sub + subs - step % subs, subs)

        @pl.loop(0, shards // pair)
        def _(c):
            queries = jnp.concatenate(
                [query_ref[c * pair + e, :span] for e in range(pair)], axis=0
            )
            scores = dot_nt(embedded[...], queries)
            best = jnp.max(scores.reshape(passages, block, pair * span), axis=1)
            best = jnp.where(counts > 0, best, -3e38)
            for e in range(pair):
                device = (group * shards + c * pair + e) * subs + sub
                out_ref[device] = best[:, e * span : (e + 1) * span]


def score(lists, replies, residuals, queries, span):
    passages, block, width = residuals.shape
    devices = len(queries) * queries[0].shape[0]
    return pl.pallas_call(
        functools.partial(score_kernel, span),
        out_shape=jax.ShapeDtypeStruct((devices, passages, span), F32),
        in_specs=[SMEM, VMEM, VMEM] + [VMEM] * len(queries),
        out_specs=VMEM,
        scratch_shapes=[
            pltpu.VMEM((replies.shape[0], width), F32),
            pltpu.VMEM((passages * block + UNROLL, width), F32),
            pltpu.VMEM((passages * block, width), BF16),
        ],
        compiler_params=pltpu.CompilerParams(vmem_limit_bytes=24 * MIB),
    )(lists, replies, residuals, *queries)


def pick_kernel(tokens, location_ref, candidates_ref, best_ref, out_ref):
    owned, listed = candidates_ref.shape
    parts, slots_total, span = best_ref.shape
    blocks, width = location_ref.shape
    which = lax.broadcasted_iota(I32, (width, listed), 0)
    slot = lax.broadcasted_iota(I32, (slots_total, listed), 0)
    sums = best_ref[0]
    for g in range(1, parts):
        sums = jnp.maximum(sums, best_ref[g])
    shift = tokens // 2
    while shift:
        sums = sums + pltpu.roll(sums, span - shift, 1)
        shift //= 2
    for q in range(owned):
        named = candidates_ref[q : q + 1]
        found = jnp.zeros((2, listed), F32)
        for g in range(blocks):
            here = location_ref[g : g + 1]
            pair = jnp.concatenate([here // 256, here % 256], axis=0).astype(F32).astype(BF16)
            hit = jnp.where(which + g * width == named, 1.0, 0.0).astype(BF16)
            found = found + dot_nn(pair, hit)
        slots = (found[0:1] * 256.0 + found[1:2]).astype(I32)
        column = jnp.broadcast_to(sums[:, q * tokens : q * tokens + 1], (slots_total, listed))
        out_ref[q : q + 1] = jnp.sum(jnp.where(slot == slots, column, 0.0), axis=0, keepdims=True)


def pick(location, candidates, best, tokens):
    return pl.pallas_call(
        functools.partial(pick_kernel, tokens),
        out_shape=jax.ShapeDtypeStruct(candidates.shape, F32),
        compiler_params=pltpu.CompilerParams(vmem_limit_bytes=16 * MIB),
    )(location, candidates, best)


def turned(array, axis, shift):
    size = lax.axis_size(axis)
    return lax.ppermute(array, axis, [(i, (i + shift) % size) for i in range(size)])


def body(queries, candidates, location, lengths, centroid_ids, residual_codes, centroids, buckets):
    token_count = centroid_ids.shape[0]
    passages = lengths.shape[0]
    height = token_count // passages
    width = residual_codes.shape[1]
    shard_rows = centroids.shape[0]
    shards, subs, parts = lax.axis_size("blk"), lax.axis_size("sub"), lax.axis_size("groups")
    cap = 2 * token_count // shards // parts
    owned, tokens = queries.shape[0], queries.shape[1]
    span = owned * tokens

    sent, pos = plan(
        lengths,
        centroid_ids.reshape(passages, height),
        queries.reshape(span, width),
        shards,
        shard_rows,
        cap,
        parts,
    )
    near = lax.all_to_all(sent, "blk", split_axis=0, concat_axis=0, tiled=True)
    found = fetch(near, centroids, span, cap)
    replies = lax.all_to_all(
        found.reshape(shards, cap, width), "blk", split_axis=0, concat_axis=0, tiled=True
    )
    lists = order(pos).reshape(token_count)
    residuals = residual(
        lists,
        residual_codes.reshape(passages, height, width),
        buckets,
        block_rows(height, shards, parts),
    )
    across = [near] + [turned(near, "groups", g) for g in range(1, parts)]
    spread = []
    for array in across:
        spread += [array] + [turned(array, "sub", s) for s in range(1, subs)]
    best = score(lists, replies.reshape(shards * cap, width), residuals, spread, span)
    mine = lax.all_to_all(best, ("groups", "blk", "sub"), split_axis=0, concat_axis=0, tiled=True)
    return pick(
        location.reshape(location.shape[0] // 128, 128),
        candidates,
        mine.reshape(parts, shards * subs * passages, span),
        tokens,
    )


def solution(mesh):
    in_specs = (
        P(("groups", "blk", "sub"), None, None),
        P(("groups", "blk", "sub"), None),
        P(),
        P(("blk", "sub")),
        P(("blk", "sub")),
        P(("blk", "sub"), None),
        P("blk", None),
        P(),
    )
    out_specs = P(("groups", "blk", "sub"), None)
    return jax.shard_map(body, mesh=mesh, in_specs=in_specs, out_specs=out_specs, check_vma=False)
```

```python
import functools

import jax
import jax.numpy as jnp
from jax import lax
from jax.experimental import pallas as pl
from jax.experimental.pallas import tpu as pltpu
from jax.sharding import PartitionSpec as P

F32 = jnp.float32
BF16 = jnp.bfloat16
I32 = jnp.int32
MIB = 1 << 20
UNROLL = 16
TILE = 16
TOKEN_AT = 12
COUNT_AT = 20
SMEM = pl.BlockSpec(memory_space=pltpu.SMEM)
VMEM = pl.BlockSpec(memory_space=pltpu.VMEM)
HBM = pl.BlockSpec(memory_space=pl.ANY)


def dot_nt(a, b):
    return lax.dot_general(a, b, (((1,), (1,)), ((), ())), preferred_element_type=F32)


def dot_nn(a, b):
    return lax.dot_general(a, b, (((1,), (0,)), ((), ())), preferred_element_type=F32)


def plan_kernel(
    shards, shard_rows, cap, parts, lengths_hbm, ids_hbm, queries_hbm, sent_ref, pos_ref,
    lengths_ref, ids_ref, queries_ref, sems,
):
    copies = [
        pltpu.make_async_copy(lengths_hbm, lengths_ref, sems.at[0]),
        pltpu.make_async_copy(ids_hbm, ids_ref, sems.at[1]),
        pltpu.make_async_copy(queries_hbm, queries_ref, sems.at[2]),
    ]
    for copy in copies:
        copy.start()
    for copy in copies:
        copy.wait()
    passages, height = ids_ref.shape
    span = queries_ref.shape[0]
    part = lax.axis_index("groups")
    ids = ids_ref[...]
    owner = ids // shard_rows
    offset = ids - owner * shard_rows
    row = lax.broadcasted_iota(I32, (passages, height), 0)
    lane = lax.broadcasted_iota(I32, (passages, height), 1)
    limit = jnp.zeros((passages, height), I32)
    for p in range(passages):
        limit = jnp.where(row == p, lengths_ref[p], limit)
    owner = jnp.where(lane < limit, owner, shards)
    mask = jnp.concatenate([jnp.where(owner == b, 1.0, 0.0) for b in range(shards)], axis=0)
    mask16 = mask.astype(BF16)
    k = lax.broadcasted_iota(I32, (height, height), 0)
    l = lax.broadcasted_iota(I32, (height, height), 1)
    inside = dot_nn(mask16, jnp.where(k < l, 1.0, 0.0).astype(BF16))
    totals = dot_nn(mask16, jnp.ones((height, height), BF16))
    full = shards * passages
    r = lax.broadcasted_iota(I32, (full, full), 0)
    c = lax.broadcasted_iota(I32, (full, full), 1)
    same = r // passages == c // passages
    ahead = dot_nn(jnp.where(same & (c < r), 1.0, 0.0).astype(BF16), totals.astype(BF16))
    place = (inside + ahead) * mask
    rank = jnp.zeros((passages, height), F32)
    for b in range(shards):
        rank = rank + place[b * passages : (b + 1) * passages]
    rank = rank.astype(I32)
    mine = (lane < limit) & (rank % parts == part)
    rank = rank // parts
    pos_ref[...] = jnp.where(mine, owner * cap + rank, -1)
    per = list_rows(cap, height)
    list_row = jnp.where(mine, owner * per + rank // height, -1)
    list_lane = rank % height
    high = (offset // 256).astype(F32)
    low = (offset % 256).astype(F32)
    rows = shards * per
    out_row = lax.broadcasted_iota(I32, (rows, height), 0)
    at_lane = lax.broadcasted_iota(I32, (height, height), 0)
    sums = jnp.zeros((rows, 2 * height), F32)
    for p in range(passages):
        here = jnp.where(out_row == list_row[p : p + 1], 1.0, 0.0).astype(BF16)
        hit = at_lane == list_lane[p : p + 1]
        values = jnp.concatenate(
            [jnp.where(hit, high[p : p + 1], 0.0), jnp.where(hit, low[p : p + 1], 0.0)], axis=0
        ).astype(BF16)
        sums = sums + dot_nt(here, values)
    queries = queries_ref[...]
    extra = message_rows(cap, height)
    for b in range(shards):
        total = jnp.sum(totals[b * passages : (b + 1) * passages], axis=0, keepdims=True)
        share = (total.astype(I32) + (parts - 1 - part)) // parts
        sent_ref[b, :span] = queries
        sent_ref[b, span:] = jnp.concatenate(
            [
                sums[b * per : (b + 1) * per, :height],
                sums[b * per : (b + 1) * per, height:],
                share.astype(F32),
                jnp.zeros((extra - 2 * per - 1, height), F32),
            ],
            axis=0,
        ).astype(BF16)


def list_rows(cap, lanes):
    return (cap + lanes - 1) // lanes


def message_rows(cap, lanes):
    return (2 * list_rows(cap, lanes) + TILE) // TILE * TILE


def plan(lengths, ids, queries, shards, shard_rows, cap, parts):
    passages, height = ids.shape
    span = queries.shape[0]
    return pl.pallas_call(
        functools.partial(plan_kernel, shards, shard_rows, cap, parts),
        out_shape=(
            jax.ShapeDtypeStruct((shards, span + message_rows(cap, height), height), BF16),
            jax.ShapeDtypeStruct((passages, height), I32),
        ),
        in_specs=[HBM, HBM, HBM],
        out_specs=(VMEM, VMEM),
        scratch_shapes=[
            pltpu.SMEM(lengths.shape, I32),
            pltpu.VMEM(ids.shape, I32),
            pltpu.VMEM(queries.shape, BF16),
            pltpu.SemaphoreType.DMA((3,)),
        ],
        compiler_params=pltpu.CompilerParams(vmem_limit_bytes=56 * MIB),
    )(lengths, ids, queries)


def block_rows(height, shards, parts):
    most = min(height, (height + shards * (parts - 1)) // parts)
    return (most + 7) // 8 * 8


def prepare_kernel(pos_ref, codes_ref, buckets_ref, list_ref, residual_ref, flat, picked, sems):
    passages, height = pos_ref.shape
    block, width = residual_ref.shape[1:]
    pos = pos_ref[...]
    mine = jnp.where(pos >= 0, 1.0, 0.0).astype(BF16)
    k = lax.broadcasted_iota(I32, (height, height), 0)
    l = lax.broadcasted_iota(I32, (height, height), 1)
    rank = dot_nn(mine, jnp.where(k < l, 1.0, 0.0).astype(BF16))
    total = dot_nn(mine, jnp.ones((height, height), BF16)).astype(I32)
    rank = jnp.where(pos >= 0, rank.astype(I32), -1)
    high = (pos // 256).astype(F32)
    low = (pos % 256).astype(F32)
    token = lax.broadcasted_iota(I32, (1, height), 1).astype(F32)
    for p in range(passages):
        hit = jnp.where(k == rank[p : p + 1], 1.0, 0.0).astype(BF16)
        values = jnp.concatenate([high[p : p + 1], low[p : p + 1], token], axis=0).astype(BF16)
        found = dot_nt(values, hit).astype(I32)
        list_ref[p : p + 1] = (
            found[0:1] * 256
            + found[1:2]
            + found[2:3] * (1 << TOKEN_AT)
            + total[p : p + 1] * (1 << COUNT_AT)
        )
    copies = [
        pltpu.make_async_copy(list_ref.at[p], flat.at[pl.ds(p * height, height)], sems.at[p])
        for p in range(passages)
    ]
    for copy in copies:
        copy.start()
    for copy in copies:
        copy.wait()

    @pl.loop(0, passages)
    def _(p):
        count = flat[p * height] >> COUNT_AT

        @pl.loop(0, (count + UNROLL - 1) // UNROLL)
        def _(i):
            at = pl.multiple_of(i * UNROLL, UNROLL)
            for u in range(UNROLL):
                token = (flat[p * height + at + u] >> TOKEN_AT) & ((1 << COUNT_AT - TOKEN_AT) - 1)
                picked[pl.ds(at + u, 1)] = codes_ref[p, pl.ds(token, 1)]

        codes = picked[:block]
        residual_ref[p] = jnp.where(
            codes == 0,
            buckets_ref[0:1],
            jnp.where(
                codes == 1,
                buckets_ref[1:2],
                jnp.where(codes == 2, buckets_ref[2:3], buckets_ref[3:4]),
            ),
        )


def prepare(pos, codes, buckets, block):
    passages, height, width = codes.shape
    return pl.pallas_call(
        prepare_kernel,
        out_shape=(
            jax.ShapeDtypeStruct((passages, height), I32),
            jax.ShapeDtypeStruct((passages, block, width), F32),
        ),
        in_specs=[VMEM, VMEM, VMEM],
        out_specs=(VMEM, VMEM),
        scratch_shapes=[
            pltpu.SMEM((passages * height,), I32),
            pltpu.VMEM((block + UNROLL, width), I32),
            pltpu.SemaphoreType.DMA((passages,)),
        ],
        compiler_params=pltpu.CompilerParams(vmem_limit_bytes=56 * MIB),
    )(pos, codes, buckets)


def fetch_kernel(
    span, shard_rows, cap, received_ref, table_hbm, after_ref, out_ref, table_ref, ask, asked, stage, sems, sem
):
    shards = received_ref.shape[0]
    height = received_ref.shape[2]
    width = table_ref.shape[1]
    per = list_rows(cap, height)
    load = pltpu.make_async_copy(table_hbm, table_ref, sem)
    load.start()
    copies = []
    for d in range(shards):
        message = received_ref[d, span:].astype(F32)
        count = message[2 * per : 2 * per + 1].astype(I32)
        offset = (message[:per] * 256.0 + message[per : 2 * per]).astype(I32)
        ask[d * per : (d + 1) * per] = offset + count * shard_rows
    for r in range(shards * per):
        copies.append(
            pltpu.make_async_copy(ask.at[r], asked.at[pl.ds(r * height, height)], sems.at[r])
        )
    for copy in copies:
        copy.start()
    for copy in copies:
        copy.wait()
    line = lax.broadcasted_iota(I32, (8, width), 0)
    low_bits = TILE - 1
    near_bits = shard_rows - TILE
    load.wait()

    @pl.loop(0, shards)
    def _(d):
        base = d * (per * height)
        count = asked[base] // shard_rows

        @pl.loop(0, (count + TILE - 1) // TILE)
        def _(i):
            at = pl.multiple_of(base + i * TILE, TILE)
            for u in range(TILE):
                near = pl.multiple_of(asked[at + u] & near_bits, TILE)
                stage[u * TILE : (u + 1) * TILE] = table_ref[pl.ds(near, TILE)].astype(F32)
            halves = []
            for h in range(0, TILE, 8):
                half = jnp.zeros((8, width), F32)
                for u in range(h, h + 8):
                    row = stage[pl.ds(u * TILE + (asked[at + u] & low_bits), 1)]
                    half = jnp.where(line == u - h, row, half)
                halves.append(half)
            to = pl.multiple_of(d * cap + i * TILE, TILE)
            out_ref[pl.ds(to, TILE)] = jnp.concatenate(halves, axis=0).astype(BF16)


def fetch(received, table, after, span, cap):
    shard_rows, width = table.shape
    shards, _, height = received.shape
    rows = shards * list_rows(cap, height)
    assert shard_rows & (shard_rows - 1) == 0
    return pl.pallas_call(
        functools.partial(fetch_kernel, span, shard_rows, cap),
        out_shape=jax.ShapeDtypeStruct((shards * cap, width), BF16),
        in_specs=[VMEM, HBM, HBM],
        out_specs=VMEM,
        scratch_shapes=[
            pltpu.VMEM(table.shape, table.dtype),
            pltpu.VMEM((rows, height), I32),
            pltpu.SMEM((rows * height,), I32),
            pltpu.VMEM((TILE * TILE, width), F32),
            pltpu.SemaphoreType.DMA((rows,)),
            pltpu.SemaphoreType.DMA,
        ],
        compiler_params=pltpu.CompilerParams(vmem_limit_bytes=56 * MIB),
    )(received, table, after)


def score_kernel(span, list_ref, replies_ref, residual_ref, *refs):
    passages, block, width = residual_ref.shape
    *query_refs, out_ref, wide, tile, embedded = refs
    groups, subs = lax.axis_size("groups"), lax.axis_size("sub")
    own_group, own_sub = lax.axis_index("groups"), lax.axis_index("sub")
    shards = query_refs[0].shape[0]
    height = list_ref.shape[0] // passages
    pair = 2 if shards % 2 == 0 else 1
    ahead = 4 if shards % (4 * pair) == 0 else 1

    @pl.loop(0, replies_ref.shape[0] // 256)
    def _(i):
        at = pl.multiple_of(i * 256, 256)
        wide[pl.ds(at, 256)] = replies_ref[pl.ds(at, 256)].astype(F32)

    @pl.loop(0, passages)
    def _(p):
        count = list_ref[p * height] >> COUNT_AT

        @pl.loop(0, (count + UNROLL - 1) // UNROLL)
        def _(i):
            at = pl.multiple_of(i * UNROLL, UNROLL)
            for u in range(UNROLL):
                place = list_ref[p * height + at + u] & ((1 << TOKEN_AT) - 1)
                tile[pl.ds(p * block + at + u, 1)] = wide[pl.ds(place, 1)]

    line = lax.broadcasted_iota(I32, (block, width), 0)
    here = lax.broadcasted_iota(I32, (passages, pair * span), 0)
    counts = jnp.zeros((passages, pair * span), I32)
    for p in range(0, passages, 2):
        both = []
        for q in (p, p + 1):
            count = list_ref[q * height] >> COUNT_AT
            counts = jnp.where(here == q, count, counts)
            rows = tile[q * block : (q + 1) * block] + residual_ref[q]
            both.append(jnp.where(line < count, rows, rows[0:1]))
        embedded[p * block : (p + 2) * block] = jnp.concatenate(both, axis=0).astype(BF16)

    for step, query_ref in enumerate(query_refs):
        group = lax.rem(own_group + groups - step // subs, groups)
        sub = lax.rem(own_sub + subs - step % subs, subs)

        @pl.loop(0, shards // (pair * ahead))
        def _(i):
            for h in range(ahead):
                c = i * ahead + h
                queries = jnp.concatenate(
                    [query_ref[c * pair + e, :span] for e in range(pair)], axis=0
                )
                scores = dot_nt(embedded[...], queries)
                best = jnp.max(scores.reshape(passages, block, pair * span), axis=1)
                best = jnp.where(counts > 0, best, -3e38)
                for e in range(pair):
                    device = (group * shards + c * pair + e) * subs + sub
                    out_ref[device] = best[:, e * span : (e + 1) * span]


def score(lists, replies, residuals, queries, span):
    passages, block, width = residuals.shape
    devices = len(queries) * queries[0].shape[0]
    return pl.pallas_call(
        functools.partial(score_kernel, span),
        out_shape=jax.ShapeDtypeStruct((devices, passages, span), F32),
        in_specs=[SMEM, VMEM, VMEM] + [VMEM] * len(queries),
        out_specs=VMEM,
        scratch_shapes=[
            pltpu.VMEM((replies.shape[0], width), F32),
            pltpu.VMEM((passages * block + UNROLL, width), F32),
            pltpu.VMEM((passages * block, width), BF16),
        ],
        compiler_params=pltpu.CompilerParams(vmem_limit_bytes=24 * MIB),
    )(lists, replies, residuals, *queries)


def pick_kernel(tokens, location_ref, candidates_ref, best_ref, out_ref):
    owned, listed = candidates_ref.shape
    parts, slots_total, span = best_ref.shape
    blocks, width = location_ref.shape
    which = lax.broadcasted_iota(I32, (width, listed), 0)
    slot = lax.broadcasted_iota(I32, (slots_total, listed), 0)
    sums = best_ref[0]
    for g in range(1, parts):
        sums = jnp.maximum(sums, best_ref[g])
    shift = tokens // 2
    while shift:
        sums = sums + pltpu.roll(sums, span - shift, 1)
        shift //= 2
    for q in range(owned):
        named = candidates_ref[q : q + 1]
        found = jnp.zeros((2, listed), F32)
        for g in range(blocks):
            here = location_ref[g : g + 1]
            pair = jnp.concatenate([here // 256, here % 256], axis=0).astype(F32).astype(BF16)
            hit = jnp.where(which + g * width == named, 1.0, 0.0).astype(BF16)
            found = found + dot_nn(pair, hit)
        slots = (found[0:1] * 256.0 + found[1:2]).astype(I32)
        column = jnp.broadcast_to(sums[:, q * tokens : q * tokens + 1], (slots_total, listed))
        out_ref[q : q + 1] = jnp.sum(jnp.where(slot == slots, column, 0.0), axis=0, keepdims=True)


def pick(location, candidates, best, tokens):
    return pl.pallas_call(
        functools.partial(pick_kernel, tokens),
        out_shape=jax.ShapeDtypeStruct(candidates.shape, F32),
        compiler_params=pltpu.CompilerParams(vmem_limit_bytes=16 * MIB),
    )(location, candidates, best)


def turned(array, axis, shift):
    size = lax.axis_size(axis)
    return lax.ppermute(array, axis, [(i, (i + shift) % size) for i in range(size)])


def body(queries, candidates, location, lengths, centroid_ids, residual_codes, centroids, buckets):
    token_count = centroid_ids.shape[0]
    passages = lengths.shape[0]
    height = token_count // passages
    width = residual_codes.shape[1]
    shard_rows = centroids.shape[0]
    shards, subs, parts = lax.axis_size("blk"), lax.axis_size("sub"), lax.axis_size("groups")
    cap = 2 * token_count // shards // parts
    owned, tokens = queries.shape[0], queries.shape[1]
    span = owned * tokens

    sent, pos = plan(
        lengths,
        centroid_ids.reshape(passages, height),
        queries.reshape(span, width),
        shards,
        shard_rows,
        cap,
        parts,
    )
    near = lax.all_to_all(sent, "blk", split_axis=0, concat_axis=0, tiled=True)
    lists, residuals = prepare(
        pos,
        residual_codes.reshape(passages, height, width),
        buckets,
        block_rows(height, shards, parts),
    )
    found = fetch(near, centroids, residuals, span, cap)
    replies = lax.all_to_all(
        found.reshape(shards, cap, width), "blk", split_axis=0, concat_axis=0, tiled=True
    )
    across = [near] + [turned(near, "groups", g) for g in range(1, parts)]
    spread = []
    for array in across:
        spread += [array] + [turned(array, "sub", s) for s in range(1, subs)]
    best = score(lists.reshape(token_count), replies.reshape(shards * cap, width), residuals, spread, span)
    mine = lax.all_to_all(best, ("groups", "blk", "sub"), split_axis=0, concat_axis=0, tiled=True)
    return pick(
        location.reshape(location.shape[0] // 128, 128),
        candidates,
        mine.reshape(parts, shards * subs * passages, span),
        tokens,
    )


def solution(mesh):
    in_specs = (
        P(("groups", "blk", "sub"), None, None),
        P(("groups", "blk", "sub"), None),
        P(),
        P(("blk", "sub")),
        P(("blk", "sub")),
        P(("blk", "sub"), None),
        P("blk", None),
        P(),
    )
    out_specs = P(("groups", "blk", "sub"), None)
    return jax.shard_map(body, mesh=mesh, in_specs=in_specs, out_specs=out_specs, check_vma=False)
```

```python
import functools

import jax
import jax.numpy as jnp
from jax import lax
from jax.experimental import pallas as pl
from jax.experimental.pallas import tpu as pltpu
from jax.sharding import PartitionSpec as P

F32 = jnp.float32
BF16 = jnp.bfloat16
I32 = jnp.int32
MIB = 1 << 20
UNROLL = 16
TILE = 16
TOKEN_AT = 12
COUNT_AT = 20
SMEM = pl.BlockSpec(memory_space=pltpu.SMEM)
VMEM = pl.BlockSpec(memory_space=pltpu.VMEM)
HBM = pl.BlockSpec(memory_space=pl.ANY)


def dot_nt(a, b):
    return lax.dot_general(a, b, (((1,), (1,)), ((), ())), preferred_element_type=F32)


def dot_nn(a, b):
    return lax.dot_general(a, b, (((1,), (0,)), ((), ())), preferred_element_type=F32)


def plan_kernel(
    shards, shard_rows, cap, parts, lengths_hbm, ids_hbm, queries_hbm, sent_ref, pos_ref,
    lengths_ref, ids_ref, queries_ref, sems,
):
    copies = [
        pltpu.make_async_copy(lengths_hbm, lengths_ref, sems.at[0]),
        pltpu.make_async_copy(ids_hbm, ids_ref, sems.at[1]),
        pltpu.make_async_copy(queries_hbm, queries_ref, sems.at[2]),
    ]
    for copy in copies:
        copy.start()
    for copy in copies:
        copy.wait()
    passages, height = ids_ref.shape
    span = queries_ref.shape[0]
    part = lax.axis_index("groups")
    ids = ids_ref[...]
    owner = ids // shard_rows
    offset = ids - owner * shard_rows
    row = lax.broadcasted_iota(I32, (passages, height), 0)
    lane = lax.broadcasted_iota(I32, (passages, height), 1)
    limit = jnp.zeros((passages, height), I32)
    for p in range(passages):
        limit = jnp.where(row == p, lengths_ref[p], limit)
    owner = jnp.where(lane < limit, owner, shards)
    kind = 2 * owner + offset // (shard_rows // 2)
    kinds = 2 * shards
    mask = jnp.concatenate([jnp.where(kind == b, 1.0, 0.0) for b in range(kinds)], axis=0)
    mask16 = mask.astype(BF16)
    k = lax.broadcasted_iota(I32, (height, height), 0)
    l = lax.broadcasted_iota(I32, (height, height), 1)
    inside = dot_nn(mask16, jnp.where(k < l, 1.0, 0.0).astype(BF16))
    totals = dot_nn(mask16, jnp.ones((height, height), BF16))
    full = kinds * passages
    r = lax.broadcasted_iota(I32, (full, full), 0)
    c = lax.broadcasted_iota(I32, (full, full), 1)
    same = r // (2 * passages) == c // (2 * passages)
    ahead = dot_nn(jnp.where(same & (c < r), 1.0, 0.0).astype(BF16), totals.astype(BF16))
    place = (inside + ahead) * mask
    rank = jnp.zeros((passages, height), F32)
    sizes = []
    for b in range(kinds):
        rank = rank + place[b * passages : (b + 1) * passages]
        size = jnp.sum(totals[b * passages : (b + 1) * passages], axis=0, keepdims=True)
        sizes.append(size.astype(I32))
    rank = rank.astype(I32)
    mine = (lane < limit) & (rank % parts == part)
    rank = rank // parts
    pos_ref[...] = jnp.where(mine, owner * cap + rank, -1)
    per = list_rows(cap, height)
    list_row = jnp.where(mine, owner * per + rank // height, -1)
    list_lane = rank % height
    high = (offset // 256).astype(F32)
    low = (offset % 256).astype(F32)
    rows = shards * per
    out_row = lax.broadcasted_iota(I32, (rows, height), 0)
    at_lane = lax.broadcasted_iota(I32, (height, height), 0)
    sums = jnp.zeros((rows, 2 * height), F32)
    for p in range(passages):
        here = jnp.where(out_row == list_row[p : p + 1], 1.0, 0.0).astype(BF16)
        hit = at_lane == list_lane[p : p + 1]
        values = jnp.concatenate(
            [jnp.where(hit, high[p : p + 1], 0.0), jnp.where(hit, low[p : p + 1], 0.0)], axis=0
        ).astype(BF16)
        sums = sums + dot_nt(here, values)
    queries = queries_ref[...]
    extra = message_rows(cap, height)
    for b in range(shards):
        share = (sizes[2 * b] + sizes[2 * b + 1] + (parts - 1 - part)) // parts
        first = (sizes[2 * b] + (parts - 1 - part)) // parts
        sent_ref[b, :span] = queries
        sent_ref[b, span:] = jnp.concatenate(
            [
                sums[b * per : (b + 1) * per, :height],
                sums[b * per : (b + 1) * per, height:],
                share.astype(F32),
                first.astype(F32),
                jnp.zeros((extra - 2 * per - 2, height), F32),
            ],
            axis=0,
        ).astype(BF16)


def list_rows(cap, lanes):
    return (cap + lanes - 1) // lanes


def message_rows(cap, lanes):
    return (2 * list_rows(cap, lanes) + 1 + TILE) // TILE * TILE


def plan(lengths, ids, queries, shards, shard_rows, cap, parts):
    passages, height = ids.shape
    span = queries.shape[0]
    return pl.pallas_call(
        functools.partial(plan_kernel, shards, shard_rows, cap, parts),
        out_shape=(
            jax.ShapeDtypeStruct((shards, span + message_rows(cap, height), height), BF16),
            jax.ShapeDtypeStruct((passages, height), I32),
        ),
        in_specs=[HBM, HBM, HBM],
        out_specs=(VMEM, VMEM),
        scratch_shapes=[
            pltpu.SMEM(lengths.shape, I32),
            pltpu.VMEM(ids.shape, I32),
            pltpu.VMEM(queries.shape, BF16),
            pltpu.SemaphoreType.DMA((3,)),
        ],
        compiler_params=pltpu.CompilerParams(vmem_limit_bytes=56 * MIB),
    )(lengths, ids, queries)


def block_rows(height, shards, parts):
    most = min(height, (height + 2 * shards * (parts - 1)) // parts)
    return (most + 7) // 8 * 8


def prepare_kernel(
    pos_ref, codes_ref, buckets_ref, location_ref, candidates_ref,
    list_ref, residual_ref, slots_ref, flat, picked, sems,
):
    passages, height = pos_ref.shape
    block, width = residual_ref.shape[1:]
    pos = pos_ref[...]
    mine = jnp.where(pos >= 0, 1.0, 0.0).astype(BF16)
    k = lax.broadcasted_iota(I32, (height, height), 0)
    l = lax.broadcasted_iota(I32, (height, height), 1)
    rank = dot_nn(mine, jnp.where(k < l, 1.0, 0.0).astype(BF16))
    total = dot_nn(mine, jnp.ones((height, height), BF16)).astype(I32)
    rank = jnp.where(pos >= 0, rank.astype(I32), -1)
    high = (pos // 256).astype(F32)
    low = (pos % 256).astype(F32)
    token = lax.broadcasted_iota(I32, (1, height), 1).astype(F32)
    for p in range(passages):
        hit = jnp.where(k == rank[p : p + 1], 1.0, 0.0).astype(BF16)
        values = jnp.concatenate([high[p : p + 1], low[p : p + 1], token], axis=0).astype(BF16)
        found = dot_nt(values, hit).astype(I32)
        list_ref[p : p + 1] = (
            found[0:1] * 256
            + found[1:2]
            + found[2:3] * (1 << TOKEN_AT)
            + total[p : p + 1] * (1 << COUNT_AT)
        )
    copies = [
        pltpu.make_async_copy(list_ref.at[p], flat.at[pl.ds(p * height, height)], sems.at[p])
        for p in range(passages)
    ]
    for copy in copies:
        copy.start()
    for copy in copies:
        copy.wait()

    @pl.loop(0, passages)
    def _(p):
        count = flat[p * height] >> COUNT_AT

        @pl.loop(0, (count + UNROLL - 1) // UNROLL)
        def _(i):
            at = pl.multiple_of(i * UNROLL, UNROLL)
            for u in range(UNROLL):
                token = (flat[p * height + at + u] >> TOKEN_AT) & ((1 << COUNT_AT - TOKEN_AT) - 1)
                picked[pl.ds(at + u, 1)] = codes_ref[p, pl.ds(token, 1)]

        codes = picked[:block]
        residual_ref[p] = jnp.where(
            codes == 0,
            buckets_ref[0:1],
            jnp.where(
                codes == 1,
                buckets_ref[1:2],
                jnp.where(codes == 2, buckets_ref[2:3], buckets_ref[3:4]),
            ),
        )

    owned, listed = candidates_ref.shape
    blocks, width = location_ref.shape
    which = lax.broadcasted_iota(I32, (width, listed), 0)
    for q in range(owned):
        named = candidates_ref[q : q + 1]
        found = jnp.zeros((2, listed), F32)
        for g in range(blocks):
            here = location_ref[g : g + 1]
            pair = jnp.concatenate([here // 256, here % 256], axis=0).astype(F32).astype(BF16)
            hit = jnp.where(which + g * width == named, 1.0, 0.0).astype(BF16)
            found = found + dot_nn(pair, hit)
        slots_ref[q : q + 1] = (found[0:1] * 256.0 + found[1:2]).astype(I32)


def prepare(pos, codes, buckets, location, candidates, block):
    passages, height, width = codes.shape
    return pl.pallas_call(
        prepare_kernel,
        out_shape=(
            jax.ShapeDtypeStruct((passages, height), I32),
            jax.ShapeDtypeStruct((passages, block, width), F32),
            jax.ShapeDtypeStruct(candidates.shape, I32),
        ),
        in_specs=[VMEM] * 5,
        out_specs=(VMEM, VMEM, VMEM),
        scratch_shapes=[
            pltpu.SMEM((passages * height,), I32),
            pltpu.VMEM((block + UNROLL, width), I32),
            pltpu.SemaphoreType.DMA((passages,)),
        ],
        compiler_params=pltpu.CompilerParams(vmem_limit_bytes=56 * MIB),
    )(pos, codes, buckets, location, candidates)


def fetch_kernel(
    span, cap, received_hbm, table_hbm, after_ref, out_ref,
    front, back, message, ask, asked, even, odd, load_sems, sems, sem,
):
    shards, _, height = received_hbm.shape
    half_tiles, _, width = front.shape
    per = list_rows(cap, height)
    rows = shards * per
    receive = pltpu.make_async_copy(
        received_hbm.at[:, pl.ds(span, message.shape[1])], message, sem
    )
    receive.start()
    loads = [
        pltpu.make_async_copy(table_hbm.at[pl.ds(h * half_tiles, half_tiles)], table, load_sems.at[h])
        for h, table in enumerate((front, back))
    ]
    loads[0].start()
    receive.wait()
    lane = lax.broadcasted_iota(I32, (1, height), 1)
    sizes = jnp.zeros((1, height), F32)
    for d in range(shards):
        lists = message[d].astype(F32)
        sizes = jnp.where(lane == d, lists[2 * per : 2 * per + 1], sizes)
        sizes = jnp.where(lane == d + shards, lists[2 * per + 1 : 2 * per + 2], sizes)
        offset = (lists[:per] * 256.0 + lists[per : 2 * per]).astype(I32)
        ask[d * per : (d + 1) * per] = (offset // TILE) & (half_tiles - 1)
        ask[rows + d * per : rows + (d + 1) * per] = offset & (TILE - 1)
    ask[2 * rows : 2 * rows + 1] = sizes.astype(I32)
    copies = [
        pltpu.make_async_copy(ask.at[r], asked.at[pl.ds(r * height, height)], sems.at[r])
        for r in range(2 * rows + 1)
    ]
    for copy in copies:
        copy.start()
    for copy in copies:
        copy.wait()
    loads[1].start()
    line = lax.broadcasted_iota(I32, (8, width), 0)

    for h, table in enumerate((front, back)):
        loads[h].wait()

        @pl.loop(0, shards)
        def _(d):
            base = d * (per * height)
            count = asked[2 * rows * height + d]
            first = asked[2 * rows * height + shards + d]
            begin = 0 if h == 0 else first // TILE
            end = ((first if h == 0 else count) + TILE - 1) // TILE

            @pl.loop(begin, end)
            def _(i):
                at = pl.multiple_of(base + i * TILE, TILE)
                low_at = pl.multiple_of(at + rows * height, TILE)
                to = pl.multiple_of(d * cap + i * TILE, TILE)
                stages = (even, odd)
                for g, stage in enumerate(stages):
                    for u in range(8):
                        stage[u * TILE : (u + 1) * TILE] = table[asked[at + 8 * g + u]].astype(F32)
                if h == 0:
                    halves = [jnp.zeros((8, width), F32)] * 2
                else:
                    old = out_ref[pl.ds(to, TILE)].astype(F32)
                    halves = [old[:8], old[8:]]
                for g, stage in enumerate(stages):
                    for u in range(8):
                        row = stage[pl.ds(u * TILE + asked[low_at + 8 * g + u], 1)]
                        here = line == u
                        if h == 1:
                            here = here & (line + (i * TILE + 8 * g) >= first)
                        halves[g] = jnp.where(here, row, halves[g])
                out_ref[pl.ds(to, TILE)] = jnp.concatenate(halves, axis=0).astype(BF16)


def fetch(received, table, after, span, cap):
    shard_rows, width = table.shape
    shards, length, height = received.shape
    rows = shards * list_rows(cap, height)
    assert shard_rows & (shard_rows - 1) == 0
    half = (shard_rows // TILE // 2, TILE, width)
    ask_rows = (2 * rows + 8) // 8 * 8
    return pl.pallas_call(
        functools.partial(fetch_kernel, span, cap),
        out_shape=jax.ShapeDtypeStruct((shards * cap, width), BF16),
        in_specs=[HBM, HBM, HBM],
        out_specs=VMEM,
        scratch_shapes=[
            pltpu.VMEM(half, table.dtype),
            pltpu.VMEM(half, table.dtype),
            pltpu.VMEM((shards, length - span, height), BF16),
            pltpu.VMEM((ask_rows, height), I32),
            pltpu.SMEM((ask_rows * height,), I32),
            pltpu.VMEM((8 * TILE, width), F32),
            pltpu.VMEM((8 * TILE, width), F32),
            pltpu.SemaphoreType.DMA((2,)),
            pltpu.SemaphoreType.DMA((2 * rows + 1,)),
            pltpu.SemaphoreType.DMA,
        ],
        compiler_params=pltpu.CompilerParams(vmem_limit_bytes=56 * MIB),
    )(received, table.reshape(shard_rows // TILE, TILE, width), after)


def score_kernel(span, list_ref, replies_ref, residual_hbm, *refs):
    passages, block, width = residual_hbm.shape
    *query_refs, out_ref, wide, tile, embedded, residual_ref, sem = refs
    load = pltpu.make_async_copy(residual_hbm, residual_ref, sem)
    load.start()
    groups, subs = lax.axis_size("groups"), lax.axis_size("sub")
    own_group, own_sub = lax.axis_index("groups"), lax.axis_index("sub")
    shards = query_refs[0].shape[0]
    height = list_ref.shape[0] // passages
    pair = 2 if shards % 2 == 0 else 1
    ahead = 4 if shards % (4 * pair) == 0 else 1

    @pl.loop(0, replies_ref.shape[0] // 256)
    def _(i):
        at = pl.multiple_of(i * 256, 256)
        wide[pl.ds(at, 256)] = replies_ref[pl.ds(at, 256)].astype(F32)

    @pl.loop(0, passages)
    def _(p):
        count = list_ref[p * height] >> COUNT_AT

        @pl.loop(0, (count + UNROLL - 1) // UNROLL)
        def _(i):
            at = pl.multiple_of(i * UNROLL, UNROLL)
            for u in range(UNROLL):
                place = list_ref[p * height + at + u] & ((1 << TOKEN_AT) - 1)
                tile[pl.ds(p * block + at + u, 1)] = wide[pl.ds(place, 1)]

    load.wait()
    line = lax.broadcasted_iota(I32, (block, width), 0)
    here = lax.broadcasted_iota(I32, (passages, pair * span), 0)
    counts = jnp.zeros((passages, pair * span), I32)
    for p in range(0, passages, 2):
        both = []
        for q in (p, p + 1):
            count = list_ref[q * height] >> COUNT_AT
            counts = jnp.where(here == q, count, counts)
            rows = tile[q * block : (q + 1) * block] + residual_ref[q]
            both.append(jnp.where(line < count, rows, rows[0:1]))
        embedded[p * block : (p + 2) * block] = jnp.concatenate(both, axis=0).astype(BF16)

    for step, query_ref in enumerate(query_refs):
        group = lax.rem(own_group + groups - step // subs, groups)
        sub = lax.rem(own_sub + subs - step % subs, subs)

        @pl.loop(0, shards // (pair * ahead))
        def _(i):
            for h in range(ahead):
                c = i * ahead + h
                queries = jnp.concatenate(
                    [query_ref[c * pair + e, :span] for e in range(pair)], axis=0
                )
                scores = dot_nt(embedded[...], queries)
                best = jnp.max(scores.reshape(passages, block, pair * span), axis=1)
                best = jnp.where(counts > 0, best, -3e38)
                for e in range(pair):
                    device = (group * shards + c * pair + e) * subs + sub
                    out_ref[device] = best[:, e * span : (e + 1) * span]


def score(lists, replies, residuals, queries, span):
    passages, block, width = residuals.shape
    devices = len(queries) * queries[0].shape[0]
    return pl.pallas_call(
        functools.partial(score_kernel, span),
        out_shape=jax.ShapeDtypeStruct((devices, passages, span), F32),
        in_specs=[SMEM, VMEM, HBM] + [VMEM] * len(queries),
        out_specs=VMEM,
        scratch_shapes=[
            pltpu.VMEM((replies.shape[0], width), F32),
            pltpu.VMEM((passages * block + UNROLL, width), F32),
            pltpu.VMEM((passages * block, width), BF16),
            pltpu.VMEM((passages, block, width), F32),
            pltpu.SemaphoreType.DMA,
        ],
        compiler_params=pltpu.CompilerParams(vmem_limit_bytes=24 * MIB),
    )(lists, replies, residuals, *queries)


def pick_kernel(tokens, slots_ref, best_ref, out_ref):
    owned, listed = slots_ref.shape
    parts, slots_total, span = best_ref.shape
    slot = lax.broadcasted_iota(I32, (slots_total, listed), 0)
    sums = best_ref[0]
    for g in range(1, parts):
        sums = jnp.maximum(sums, best_ref[g])
    shift = tokens // 2
    while shift:
        sums = sums + pltpu.roll(sums, span - shift, 1)
        shift //= 2
    for q in range(owned):
        column = jnp.broadcast_to(sums[:, q * tokens : q * tokens + 1], (slots_total, listed))
        chosen = jnp.where(slot == slots_ref[q : q + 1], column, 0.0)
        out_ref[q : q + 1] = jnp.sum(chosen, axis=0, keepdims=True)


def pick(slots, best, tokens):
    return pl.pallas_call(
        functools.partial(pick_kernel, tokens),
        out_shape=jax.ShapeDtypeStruct(slots.shape, F32),
        compiler_params=pltpu.CompilerParams(vmem_limit_bytes=16 * MIB),
    )(slots, best)


def turned(array, axis, shift):
    size = lax.axis_size(axis)
    return lax.ppermute(array, axis, [(i, (i + shift) % size) for i in range(size)])


def body(queries, candidates, location, lengths, centroid_ids, residual_codes, centroids, buckets):
    token_count = centroid_ids.shape[0]
    passages = lengths.shape[0]
    height = token_count // passages
    width = residual_codes.shape[1]
    shard_rows = centroids.shape[0]
    shards, subs, parts = lax.axis_size("blk"), lax.axis_size("sub"), lax.axis_size("groups")
    cap = 2 * token_count // shards // parts
    owned, tokens = queries.shape[0], queries.shape[1]
    span = owned * tokens

    sent, pos = plan(
        lengths,
        centroid_ids.reshape(passages, height),
        queries.reshape(span, width),
        shards,
        shard_rows,
        cap,
        parts,
    )
    near = lax.all_to_all(sent, "blk", split_axis=0, concat_axis=0, tiled=True)
    lists, residuals, slots = prepare(
        pos,
        residual_codes.reshape(passages, height, width),
        buckets,
        location.reshape(location.shape[0] // 128, 128),
        candidates,
        block_rows(height, shards, parts),
    )
    found = fetch(near, centroids, slots, span, cap)
    replies = lax.all_to_all(
        found.reshape(shards, cap, width), "blk", split_axis=0, concat_axis=0, tiled=True
    )
    across = [near] + [turned(near, "groups", g) for g in range(1, parts)]
    spread = []
    for array in across:
        others = [turned(array, "sub", s) for s in range(1, subs)]
        own = turned(others[-1], "sub", 1) if array is near and others else array
        spread += [own] + others
    best = score(lists.reshape(token_count), replies.reshape(shards * cap, width), residuals, spread, span)
    mine = lax.all_to_all(best, ("groups", "blk", "sub"), split_axis=0, concat_axis=0, tiled=True)
    return pick(slots, mine.reshape(parts, shards * subs * passages, span), tokens)


def solution(mesh):
    in_specs = (
        P(("groups", "blk", "sub"), None, None),
        P(("groups", "blk", "sub"), None),
        P(),
        P(("blk", "sub")),
        P(("blk", "sub")),
        P(("blk", "sub"), None),
        P("blk", None),
        P(),
    )
    out_specs = P(("groups", "blk", "sub"), None)
    return jax.shard_map(body, mesh=mesh, in_specs=in_specs, out_specs=out_specs, check_vma=False)
```

```python
import functools

import jax
import jax.numpy as jnp
from jax import lax
from jax.experimental import pallas as pl
from jax.experimental.pallas import tpu as pltpu
from jax.sharding import PartitionSpec as P

F32 = jnp.float32
BF16 = jnp.bfloat16
I32 = jnp.int32
MIB = 1 << 20
UNROLL = 16
TILE = 16
SMEM = pl.BlockSpec(memory_space=pltpu.SMEM)
VMEM = pl.BlockSpec(memory_space=pltpu.VMEM)
HBM = pl.BlockSpec(memory_space=pl.ANY)


def dot_nt(a, b):
    return lax.dot_general(a, b, (((1,), (1,)), ((), ())), preferred_element_type=F32)


def dot_nn(a, b):
    return lax.dot_general(a, b, (((1,), (0,)), ((), ())), preferred_element_type=F32)


def plan_kernel(
    shards, shard_rows, cap, parts, lengths_hbm, ids_hbm, queries_hbm, sent_ref, pos_ref,
    lengths_ref, ids_ref, queries_ref, sems,
):
    copies = [
        pltpu.make_async_copy(lengths_hbm, lengths_ref, sems.at[0]),
        pltpu.make_async_copy(ids_hbm, ids_ref, sems.at[1]),
        pltpu.make_async_copy(queries_hbm, queries_ref, sems.at[2]),
    ]
    for copy in copies:
        copy.start()
    for copy in copies[:2]:
        copy.wait()
    passages, height = ids_ref.shape
    span = queries_ref.shape[0]
    part = lax.axis_index("groups")
    ids = ids_ref[...]
    owner = ids // shard_rows
    offset = ids - owner * shard_rows
    row = lax.broadcasted_iota(I32, (passages, height), 0)
    lane = lax.broadcasted_iota(I32, (passages, height), 1)
    limit = jnp.zeros((passages, height), I32)
    for p in range(passages):
        limit = jnp.where(row == p, lengths_ref[p], limit)
    owner = jnp.where(lane < limit, owner, shards)
    kind = 2 * owner + offset // (shard_rows // 2)
    kinds = 2 * shards
    mask = jnp.concatenate([jnp.where(kind == b, 1.0, 0.0) for b in range(kinds)], axis=0)
    mask16 = mask.astype(BF16)
    k = lax.broadcasted_iota(I32, (height, height), 0)
    l = lax.broadcasted_iota(I32, (height, height), 1)
    inside = dot_nn(mask16, jnp.where(k < l, 1.0, 0.0).astype(BF16))
    totals = dot_nn(mask16, jnp.ones((height, height), BF16))
    full = kinds * passages
    r = lax.broadcasted_iota(I32, (full, full), 0)
    c = lax.broadcasted_iota(I32, (full, full), 1)
    same = r // (2 * passages) == c // (2 * passages)
    ahead = dot_nn(jnp.where(same & (c < r), 1.0, 0.0).astype(BF16), totals.astype(BF16))
    place = (inside + ahead) * mask
    rank = jnp.zeros((passages, height), F32)
    sizes = []
    for b in range(kinds):
        rank = rank + place[b * passages : (b + 1) * passages]
        size = jnp.sum(totals[b * passages : (b + 1) * passages], axis=0, keepdims=True)
        sizes.append(size.astype(I32))
    rank = rank.astype(I32)
    mine = (lane < limit) & (rank % parts == part)
    rank = rank // parts
    pos_ref[...] = jnp.where(mine, owner * cap + rank, -1)
    per = list_rows(cap, height)
    list_row = jnp.where(mine, owner * per + rank // height, -1)
    list_lane = rank % height
    high = (offset // 256).astype(F32)
    low = (offset % 256).astype(F32)
    rows = shards * per
    out_row = lax.broadcasted_iota(I32, (rows, height), 0)
    at_lane = lax.broadcasted_iota(I32, (height, height), 0)
    sums = jnp.zeros((rows, 2 * height), F32)
    for p in range(passages):
        here = jnp.where(out_row == list_row[p : p + 1], 1.0, 0.0).astype(BF16)
        hit = at_lane == list_lane[p : p + 1]
        values = jnp.concatenate(
            [jnp.where(hit, high[p : p + 1], 0.0), jnp.where(hit, low[p : p + 1], 0.0)], axis=0
        ).astype(BF16)
        sums = sums + dot_nt(here, values)
    copies[2].wait()
    queries = queries_ref[...]
    extra = message_rows(cap, height)
    for b in range(shards):
        share = (sizes[2 * b] + sizes[2 * b + 1] + (parts - 1 - part)) // parts
        first = (sizes[2 * b] + (parts - 1 - part)) // parts
        sent_ref[b, :span] = queries
        sent_ref[b, span:] = jnp.concatenate(
            [
                sums[b * per : (b + 1) * per, :height],
                sums[b * per : (b + 1) * per, height:],
                share.astype(F32),
                first.astype(F32),
                jnp.zeros((extra - 2 * per - 2, height), F32),
            ],
            axis=0,
        ).astype(BF16)


def list_rows(cap, lanes):
    return (cap + lanes - 1) // lanes


def message_rows(cap, lanes):
    return (2 * list_rows(cap, lanes) + 1 + TILE) // TILE * TILE


def plan(lengths, ids, queries, shards, shard_rows, cap, parts):
    passages, height = ids.shape
    span = queries.shape[0]
    return pl.pallas_call(
        functools.partial(plan_kernel, shards, shard_rows, cap, parts),
        out_shape=(
            jax.ShapeDtypeStruct((shards, span + message_rows(cap, height), height), BF16),
            jax.ShapeDtypeStruct((passages, height), I32),
        ),
        in_specs=[HBM, HBM, HBM],
        out_specs=(VMEM, VMEM),
        scratch_shapes=[
            pltpu.SMEM(lengths.shape, I32),
            pltpu.VMEM(ids.shape, I32),
            pltpu.VMEM(queries.shape, BF16),
            pltpu.SemaphoreType.DMA((3,)),
        ],
        compiler_params=pltpu.CompilerParams(vmem_limit_bytes=56 * MIB),
    )(lengths, ids, queries)


def block_rows(height, shards, parts):
    most = min(height, (height + 2 * shards * (parts - 1)) // parts)
    return (most + 7) // 8 * 8


def prepare_kernel(
    pos_ref, codes_ref, buckets_ref, location_ref, candidates_ref,
    list_ref, residual_ref, slots_ref, tokens, flat, picked, sems,
):
    passages, height = pos_ref.shape
    block, width = residual_ref.shape[1:]
    pos = pos_ref[...]
    mine = jnp.where(pos >= 0, 1.0, 0.0).astype(BF16)
    k = lax.broadcasted_iota(I32, (height, height), 0)
    l = lax.broadcasted_iota(I32, (height, height), 1)
    rank = dot_nn(mine, jnp.where(k < l, 1.0, 0.0).astype(BF16))
    total = dot_nn(mine, jnp.ones((height, height), BF16)).astype(I32)
    rank = jnp.where(pos >= 0, rank.astype(I32), -1)
    high = (pos // 256).astype(F32)
    low = (pos % 256).astype(F32)
    token = lax.broadcasted_iota(I32, (1, height), 1).astype(F32)
    lane = lax.broadcasted_iota(I32, (1, height), 1)
    counts = jnp.zeros((1, height), I32)
    for p in range(passages):
        hit = jnp.where(k == rank[p : p + 1], 1.0, 0.0).astype(BF16)
        values = jnp.concatenate([high[p : p + 1], low[p : p + 1], token], axis=0).astype(BF16)
        found = dot_nt(values, hit).astype(I32)
        list_ref[p : p + 1] = found[0:1] * 256 + found[1:2]
        tokens[p : p + 1] = found[2:3]
        counts = jnp.where(lane == p, total[p : p + 1], counts)
    list_ref[passages : passages + 1] = counts
    tokens[passages : passages + 1] = counts
    copies = [
        pltpu.make_async_copy(tokens.at[p], flat.at[pl.ds(p * height, height)], sems.at[p])
        for p in range(passages + 1)
    ]
    for copy in copies:
        copy.start()
    for copy in copies:
        copy.wait()

    @pl.loop(0, passages)
    def _(p):
        count = flat[passages * height + p]

        @pl.loop(0, (count + UNROLL - 1) // UNROLL)
        def _(i):
            at = pl.multiple_of(i * UNROLL, UNROLL)
            for u in range(UNROLL):
                picked[pl.ds(at + u, 1)] = codes_ref[p, pl.ds(flat[p * height + at + u], 1)]

        codes = picked[:block]
        residual_ref[p] = jnp.where(
            codes == 0,
            buckets_ref[0:1],
            jnp.where(
                codes == 1,
                buckets_ref[1:2],
                jnp.where(codes == 2, buckets_ref[2:3], buckets_ref[3:4]),
            ),
        )

    owned, listed = candidates_ref.shape
    blocks, width = location_ref.shape
    which = lax.broadcasted_iota(I32, (width, listed), 0)
    for q in range(owned):
        named = candidates_ref[q : q + 1]
        found = jnp.zeros((2, listed), F32)
        for g in range(blocks):
            here = location_ref[g : g + 1]
            pair = jnp.concatenate([here // 256, here % 256], axis=0).astype(F32).astype(BF16)
            hit = jnp.where(which + g * width == named, 1.0, 0.0).astype(BF16)
            found = found + dot_nn(pair, hit)
        slots_ref[q : q + 1] = (found[0:1] * 256.0 + found[1:2]).astype(I32)


def prepare(pos, codes, buckets, location, candidates, block):
    passages, height, width = codes.shape
    return pl.pallas_call(
        prepare_kernel,
        out_shape=(
            jax.ShapeDtypeStruct((passages + 8, height), I32),
            jax.ShapeDtypeStruct((passages, block, width), F32),
            jax.ShapeDtypeStruct(candidates.shape, I32),
        ),
        in_specs=[VMEM] * 5,
        out_specs=(VMEM, VMEM, VMEM),
        scratch_shapes=[
            pltpu.VMEM((passages + 8, height), I32),
            pltpu.SMEM(((passages + 1) * height,), I32),
            pltpu.VMEM((block + UNROLL, width), I32),
            pltpu.SemaphoreType.DMA((passages + 1,)),
        ],
        compiler_params=pltpu.CompilerParams(vmem_limit_bytes=56 * MIB),
    )(pos, codes, buckets, location, candidates)


def fetch_kernel(
    span, cap, received_hbm, table_hbm, after_ref, out_ref,
    front, back, message, ask, asked, even, odd, load_sems, sems, sem,
):
    shards, _, height = received_hbm.shape
    half_tiles, _, width = front.shape
    per = list_rows(cap, height)
    rows = shards * per
    receive = pltpu.make_async_copy(
        received_hbm.at[:, pl.ds(span, message.shape[1])], message, sem
    )
    receive.start()
    loads = [
        pltpu.make_async_copy(table_hbm.at[pl.ds(h * half_tiles, half_tiles)], table, load_sems.at[h])
        for h, table in enumerate((front, back))
    ]
    loads[0].start()
    receive.wait()
    lane = lax.broadcasted_iota(I32, (1, height), 1)
    sizes = jnp.zeros((1, height), F32)
    for d in range(shards):
        lists = message[d].astype(F32)
        sizes = jnp.where(lane == d, lists[2 * per : 2 * per + 1], sizes)
        sizes = jnp.where(lane == d + shards, lists[2 * per + 1 : 2 * per + 2], sizes)
        offset = (lists[:per] * 256.0 + lists[per : 2 * per]).astype(I32)
        ask[d * per : (d + 1) * per] = (offset // TILE) & (half_tiles - 1)
        ask[rows + d * per : rows + (d + 1) * per] = offset & (TILE - 1)
    ask[2 * rows : 2 * rows + 1] = sizes.astype(I32)
    loads[1].start()
    copies = [
        pltpu.make_async_copy(ask.at[r], asked.at[pl.ds(r * height, height)], sems.at[r])
        for r in range(2 * rows + 1)
    ]
    for copy in copies:
        copy.start()
    for copy in copies:
        copy.wait()
    line = lax.broadcasted_iota(I32, (8, width), 0)

    for h, table in enumerate((front, back)):
        loads[h].wait()

        @pl.loop(0, shards)
        def _(d):
            base = d * (per * height)
            count = asked[2 * rows * height + d]
            first = asked[2 * rows * height + shards + d]
            begin = 0 if h == 0 else first // TILE
            end = ((first if h == 0 else count) + TILE - 1) // TILE

            @pl.loop(begin, end)
            def _(i):
                at = pl.multiple_of(base + i * TILE, TILE)
                low_at = pl.multiple_of(at + rows * height, TILE)
                to = pl.multiple_of(d * cap + i * TILE, TILE)
                stages = (even, odd)
                for g, stage in enumerate(stages):
                    for u in range(8):
                        stage[u * TILE : (u + 1) * TILE] = table[asked[at + 8 * g + u]].astype(F32)
                if h == 0:
                    halves = [jnp.zeros((8, width), F32)] * 2
                else:
                    old = out_ref[pl.ds(to, TILE)].astype(F32)
                    halves = [old[:8], old[8:]]
                for g, stage in enumerate(stages):
                    for u in range(8):
                        row = stage[pl.ds(u * TILE + asked[low_at + 8 * g + u], 1)]
                        here = line == u
                        if h == 1:
                            here = here & (line + (i * TILE + 8 * g) >= first)
                        halves[g] = jnp.where(here, row, halves[g])
                out_ref[pl.ds(to, TILE)] = jnp.concatenate(halves, axis=0).astype(BF16)


def fetch(received, table, after, span, cap):
    shard_rows, width = table.shape
    shards, length, height = received.shape
    rows = shards * list_rows(cap, height)
    assert shard_rows & (shard_rows - 1) == 0
    half = (shard_rows // TILE // 2, TILE, width)
    ask_rows = (2 * rows + 8) // 8 * 8
    return pl.pallas_call(
        functools.partial(fetch_kernel, span, cap),
        out_shape=jax.ShapeDtypeStruct((shards * cap, width), BF16),
        in_specs=[HBM, HBM, HBM],
        out_specs=VMEM,
        scratch_shapes=[
            pltpu.VMEM(half, table.dtype),
            pltpu.VMEM(half, table.dtype),
            pltpu.VMEM((shards, length - span, height), BF16),
            pltpu.VMEM((ask_rows, height), I32),
            pltpu.SMEM((ask_rows * height,), I32),
            pltpu.VMEM((8 * TILE, width), F32),
            pltpu.VMEM((8 * TILE, width), F32),
            pltpu.SemaphoreType.DMA((2,)),
            pltpu.SemaphoreType.DMA((2 * rows + 1,)),
            pltpu.SemaphoreType.DMA,
        ],
        compiler_params=pltpu.CompilerParams(vmem_limit_bytes=56 * MIB),
    )(received, table.reshape(shard_rows // TILE, TILE, width), after)


def score_kernel(span, list_hbm, replies_ref, residual_hbm, *refs):
    passages, block, width = residual_hbm.shape
    *query_refs, out_ref, wide, tile, embedded, residual_ref, list_ref, sems = refs
    listing = pltpu.make_async_copy(list_hbm, list_ref, sems.at[0])
    listing.start()
    load = pltpu.make_async_copy(residual_hbm, residual_ref, sems.at[1])
    load.start()
    groups, subs = lax.axis_size("groups"), lax.axis_size("sub")
    own_group, own_sub = lax.axis_index("groups"), lax.axis_index("sub")
    shards = query_refs[0].shape[0]
    height = list_ref.shape[0] // (passages + 8)
    pair = 2 if shards % 2 == 0 else 1
    ahead = 4 if shards % (4 * pair) == 0 else 1

    @pl.loop(0, replies_ref.shape[0] // 256)
    def _(i):
        at = pl.multiple_of(i * 256, 256)
        wide[pl.ds(at, 256)] = replies_ref[pl.ds(at, 256)].astype(F32)

    listing.wait()

    @pl.loop(0, passages)
    def _(p):
        count = list_ref[passages * height + p]

        def move(at, rows):
            for u in range(rows):
                place = list_ref[p * height + at + u]
                tile[pl.ds(p * block + at + u, 1)] = wide[pl.ds(place, 1)]

        move(0, 32)

        @pl.loop(2, (count + UNROLL - 1) // UNROLL)
        def _(i):
            move(pl.multiple_of(i * UNROLL, UNROLL), UNROLL)

    load.wait()
    line = lax.broadcasted_iota(I32, (block, width), 0)
    here = lax.broadcasted_iota(I32, (passages, pair * span), 0)
    counts = jnp.zeros((passages, pair * span), I32)
    for p in range(0, passages, 2):
        both = []
        for q in (p, p + 1):
            count = list_ref[passages * height + q]
            counts = jnp.where(here == q, count, counts)
            rows = tile[q * block : (q + 1) * block] + residual_ref[q]
            both.append(jnp.where(line < count, rows, rows[0:1]))
        embedded[p * block : (p + 2) * block] = jnp.concatenate(both, axis=0).astype(BF16)

    for step, query_ref in enumerate(query_refs):
        group = lax.rem(own_group + groups - step // subs, groups)
        sub = lax.rem(own_sub + subs - step % subs, subs)

        @pl.loop(0, shards // (pair * ahead))
        def _(i):
            for h in range(ahead):
                c = i * ahead + h
                queries = jnp.concatenate(
                    [query_ref[c * pair + e, :span] for e in range(pair)], axis=0
                )
                scores = dot_nt(embedded[...], queries)
                best = jnp.max(scores.reshape(passages, block, pair * span), axis=1)
                best = jnp.where(counts > 0, best, -3e38)
                for e in range(pair):
                    device = (group * shards + c * pair + e) * subs + sub
                    out_ref[device] = best[:, e * span : (e + 1) * span]


def score(lists, replies, residuals, queries, span):
    passages, block, width = residuals.shape
    devices = len(queries) * queries[0].shape[0]
    return pl.pallas_call(
        functools.partial(score_kernel, span),
        out_shape=jax.ShapeDtypeStruct((devices, passages, span), F32),
        in_specs=[HBM, VMEM, HBM] + [VMEM] * len(queries),
        out_specs=VMEM,
        scratch_shapes=[
            pltpu.VMEM((replies.shape[0], width), F32),
            pltpu.VMEM((passages * block + UNROLL, width), F32),
            pltpu.VMEM((passages * block, width), BF16),
            pltpu.VMEM((passages, block, width), F32),
            pltpu.SMEM(lists.shape, I32),
            pltpu.SemaphoreType.DMA((2,)),
        ],
        compiler_params=pltpu.CompilerParams(vmem_limit_bytes=24 * MIB),
    )(lists, replies, residuals, *queries)


def pick_kernel(tokens, slots_ref, best_ref, out_ref):
    owned, listed = slots_ref.shape
    parts, slots_total, span = best_ref.shape
    slot = lax.broadcasted_iota(I32, (slots_total, listed), 0)
    sums = best_ref[0]
    for g in range(1, parts):
        sums = jnp.maximum(sums, best_ref[g])
    shift = tokens // 2
    while shift:
        sums = sums + pltpu.roll(sums, span - shift, 1)
        shift //= 2
    for q in range(owned):
        column = jnp.broadcast_to(sums[:, q * tokens : q * tokens + 1], (slots_total, listed))
        chosen = jnp.where(slot == slots_ref[q : q + 1], column, 0.0)
        out_ref[q : q + 1] = jnp.sum(chosen, axis=0, keepdims=True)


def pick(slots, best, tokens):
    return pl.pallas_call(
        functools.partial(pick_kernel, tokens),
        out_shape=jax.ShapeDtypeStruct(slots.shape, F32),
        compiler_params=pltpu.CompilerParams(vmem_limit_bytes=16 * MIB),
    )(slots, best)


def turned(array, axis, shift):
    size = lax.axis_size(axis)
    return lax.ppermute(array, axis, [(i, (i + shift) % size) for i in range(size)])


def body(queries, candidates, location, lengths, centroid_ids, residual_codes, centroids, buckets):
    token_count = centroid_ids.shape[0]
    passages = lengths.shape[0]
    height = token_count // passages
    width = residual_codes.shape[1]
    shard_rows = centroids.shape[0]
    shards, subs, parts = lax.axis_size("blk"), lax.axis_size("sub"), lax.axis_size("groups")
    cap = 2 * token_count // shards // parts
    owned, tokens = queries.shape[0], queries.shape[1]
    span = owned * tokens

    sent, pos = plan(
        lengths,
        centroid_ids.reshape(passages, height),
        queries.reshape(span, width),
        shards,
        shard_rows,
        cap,
        parts,
    )
    near = lax.all_to_all(sent, "blk", split_axis=0, concat_axis=0, tiled=True)
    lists, residuals, slots = prepare(
        pos,
        residual_codes.reshape(passages, height, width),
        buckets,
        location.reshape(location.shape[0] // 128, 128),
        candidates,
        block_rows(height, shards, parts),
    )
    found = fetch(near, centroids, slots, span, cap)
    replies = lax.all_to_all(
        found.reshape(shards, cap, width), "blk", split_axis=0, concat_axis=0, tiled=True
    )
    across = [near] + [turned(near, "groups", g) for g in range(1, parts)]
    spread = []
    for array in across:
        others = [turned(array, "sub", s) for s in range(1, subs)]
        own = turned(others[-1], "sub", 1) if array is near and others else array
        spread += [own] + others
    best = score(lists.reshape(lists.size), replies.reshape(shards * cap, width), residuals, spread, span)
    mine = lax.all_to_all(best, ("groups", "blk", "sub"), split_axis=0, concat_axis=0, tiled=True)
    return pick(slots, mine.reshape(parts, shards * subs * passages, span), tokens)


def solution(mesh):
    in_specs = (
        P(("groups", "blk", "sub"), None, None),
        P(("groups", "blk", "sub"), None),
        P(),
        P(("blk", "sub")),
        P(("blk", "sub")),
        P(("blk", "sub"), None),
        P("blk", None),
        P(),
    )
    out_specs = P(("groups", "blk", "sub"), None)
    return jax.shard_map(body, mesh=mesh, in_specs=in_specs, out_specs=out_specs, check_vma=False)
```

```python
import functools

import jax
import jax.numpy as jnp
from jax import lax
from jax.experimental import pallas as pl
from jax.experimental.pallas import tpu as pltpu
from jax.sharding import PartitionSpec as P

F32 = jnp.float32
BF16 = jnp.bfloat16
I32 = jnp.int32
MIB = 1 << 20
UNROLL = 16
TILE = 16
SMEM = pl.BlockSpec(memory_space=pltpu.SMEM)
VMEM = pl.BlockSpec(memory_space=pltpu.VMEM)
HBM = pl.BlockSpec(memory_space=pl.ANY)


def dot_nt(a, b):
    return lax.dot_general(a, b, (((1,), (1,)), ((), ())), preferred_element_type=F32)


def dot_nn(a, b):
    return lax.dot_general(a, b, (((1,), (0,)), ((), ())), preferred_element_type=F32)


def plan_kernel(
    shards, shard_rows, cap, parts, lengths_hbm, ids_hbm, queries_hbm, sent_ref, pos_ref,
    lengths_ref, ids_ref, queries_ref, sems,
):
    copies = [
        pltpu.make_async_copy(lengths_hbm, lengths_ref, sems.at[0]),
        pltpu.make_async_copy(ids_hbm, ids_ref, sems.at[1]),
        pltpu.make_async_copy(queries_hbm, queries_ref, sems.at[2]),
    ]
    for copy in copies:
        copy.start()
    for copy in copies[:2]:
        copy.wait()
    passages, height = ids_ref.shape
    span = queries_ref.shape[0]
    part = lax.axis_index("groups")
    ids = ids_ref[...]
    owner = ids // shard_rows
    offset = ids - owner * shard_rows
    row = lax.broadcasted_iota(I32, (passages, height), 0)
    lane = lax.broadcasted_iota(I32, (passages, height), 1)
    limit = jnp.zeros((passages, height), I32)
    for p in range(passages):
        limit = jnp.where(row == p, lengths_ref[p], limit)
    owner = jnp.where(lane < limit, owner, shards)
    kind = 2 * owner + offset // (shard_rows // 2)
    kinds = 2 * shards
    mask = jnp.concatenate([jnp.where(kind == b, 1.0, 0.0) for b in range(kinds)], axis=0)
    mask16 = mask.astype(BF16)
    k = lax.broadcasted_iota(I32, (height, height), 0)
    l = lax.broadcasted_iota(I32, (height, height), 1)
    inside = dot_nn(mask16, jnp.where(k < l, 1.0, 0.0).astype(BF16))
    totals = dot_nn(mask16, jnp.ones((height, height), BF16))
    full = kinds * passages
    r = lax.broadcasted_iota(I32, (full, full), 0)
    c = lax.broadcasted_iota(I32, (full, full), 1)
    same = r // (2 * passages) == c // (2 * passages)
    ahead = dot_nn(jnp.where(same & (c < r), 1.0, 0.0).astype(BF16), totals.astype(BF16))
    place = (inside + ahead) * mask
    rank = jnp.zeros((passages, height), F32)
    sizes = []
    for b in range(kinds):
        rank = rank + place[b * passages : (b + 1) * passages]
        size = jnp.sum(totals[b * passages : (b + 1) * passages], axis=0, keepdims=True)
        sizes.append(size.astype(I32))
    rank = rank.astype(I32)
    mine = (lane < limit) & (rank % parts == part)
    rank = rank // parts
    pos_ref[...] = jnp.where(mine, owner * cap + rank, -1)
    per = list_rows(cap, height)
    list_row = jnp.where(mine, owner * per + rank // height, -1)
    list_lane = rank % height
    high = (offset // 256).astype(F32)
    low = (offset % 256).astype(F32)
    rows = shards * per
    out_row = lax.broadcasted_iota(I32, (rows, height), 0)
    at_lane = lax.broadcasted_iota(I32, (height, height), 0)
    sums = jnp.zeros((rows, 2 * height), F32)
    for p in range(passages):
        here = jnp.where(out_row == list_row[p : p + 1], 1.0, 0.0).astype(BF16)
        hit = at_lane == list_lane[p : p + 1]
        values = jnp.concatenate(
            [jnp.where(hit, high[p : p + 1], 0.0), jnp.where(hit, low[p : p + 1], 0.0)], axis=0
        ).astype(BF16)
        sums = sums + dot_nt(here, values)
    copies[2].wait()
    queries = queries_ref[...]
    extra = message_rows(cap, height)
    for b in range(shards):
        share = (sizes[2 * b] + sizes[2 * b + 1] + (parts - 1 - part)) // parts
        first = (sizes[2 * b] + (parts - 1 - part)) // parts
        sent_ref[b, :span] = queries
        sent_ref[b, span:] = jnp.concatenate(
            [
                sums[b * per : (b + 1) * per, :height],
                sums[b * per : (b + 1) * per, height:],
                share.astype(F32),
                first.astype(F32),
                jnp.zeros((extra - 2 * per - 2, height), F32),
            ],
            axis=0,
        ).astype(BF16)


def list_rows(cap, lanes):
    return (cap + lanes - 1) // lanes


def message_rows(cap, lanes):
    return (2 * list_rows(cap, lanes) + 1 + TILE) // TILE * TILE


def plan(lengths, ids, queries, shards, shard_rows, cap, parts):
    passages, height = ids.shape
    span = queries.shape[0]
    return pl.pallas_call(
        functools.partial(plan_kernel, shards, shard_rows, cap, parts),
        out_shape=(
            jax.ShapeDtypeStruct((shards, span + message_rows(cap, height), height), BF16),
            jax.ShapeDtypeStruct((passages, height), I32),
        ),
        in_specs=[HBM, HBM, HBM],
        out_specs=(VMEM, VMEM),
        scratch_shapes=[
            pltpu.SMEM(lengths.shape, I32),
            pltpu.VMEM(ids.shape, I32),
            pltpu.VMEM(queries.shape, BF16),
            pltpu.SemaphoreType.DMA((3,)),
        ],
        compiler_params=pltpu.CompilerParams(vmem_limit_bytes=56 * MIB),
    )(lengths, ids, queries)


def block_rows(height, shards, parts):
    most = min(height, (height + 2 * shards * (parts - 1)) // parts)
    return (most + 7) // 8 * 8


def prepare_kernel(
    pos_ref, codes_ref, buckets_ref, location_ref, candidates_ref,
    list_ref, residual_ref, slots_ref, tokens, flat, picked, sems,
):
    passages, height = pos_ref.shape
    block, width = residual_ref.shape[1:]
    pos = pos_ref[...]
    mine = jnp.where(pos >= 0, 1.0, 0.0).astype(BF16)
    k = lax.broadcasted_iota(I32, (height, height), 0)
    l = lax.broadcasted_iota(I32, (height, height), 1)
    rank = dot_nn(mine, jnp.where(k < l, 1.0, 0.0).astype(BF16))
    total = dot_nn(mine, jnp.ones((height, height), BF16)).astype(I32)
    rank = jnp.where(pos >= 0, rank.astype(I32), -1)
    high = (pos // 256).astype(F32)
    low = (pos % 256).astype(F32)
    token = lax.broadcasted_iota(I32, (1, height), 1).astype(F32)
    lane = lax.broadcasted_iota(I32, (1, height), 1)
    counts = jnp.zeros((1, height), I32)
    for p in range(passages):
        hit = jnp.where(k == rank[p : p + 1], 1.0, 0.0).astype(BF16)
        values = jnp.concatenate([high[p : p + 1], low[p : p + 1], token], axis=0).astype(BF16)
        found = dot_nt(values, hit).astype(I32)
        list_ref[p : p + 1] = found[0:1] * 256 + found[1:2]
        tokens[p : p + 1] = found[2:3]
        counts = jnp.where(lane == p, total[p : p + 1], counts)
    list_ref[passages : passages + 1] = counts
    tokens[passages : passages + 1] = counts
    copies = [
        pltpu.make_async_copy(tokens.at[p], flat.at[pl.ds(p * height, height)], sems.at[p])
        for p in range(passages + 1)
    ]
    for copy in copies:
        copy.start()
    for copy in copies:
        copy.wait()

    @pl.loop(0, passages)
    def _(p):
        count = flat[passages * height + p]

        @pl.loop(0, (count + UNROLL - 1) // UNROLL)
        def _(i):
            at = pl.multiple_of(i * UNROLL, UNROLL)
            for u in range(UNROLL):
                picked[pl.ds(at + u, 1)] = codes_ref[p, pl.ds(flat[p * height + at + u], 1)]

        codes = picked[:block]
        residual_ref[p] = jnp.where(
            codes == 0,
            buckets_ref[0:1],
            jnp.where(
                codes == 1,
                buckets_ref[1:2],
                jnp.where(codes == 2, buckets_ref[2:3], buckets_ref[3:4]),
            ),
        )

    owned, listed = candidates_ref.shape
    blocks, width = location_ref.shape
    which = lax.broadcasted_iota(I32, (width, listed), 0)
    for q in range(owned):
        named = candidates_ref[q : q + 1]
        found = jnp.zeros((2, listed), F32)
        for g in range(blocks):
            here = location_ref[g : g + 1]
            pair = jnp.concatenate([here // 256, here % 256], axis=0).astype(F32).astype(BF16)
            hit = jnp.where(which + g * width == named, 1.0, 0.0).astype(BF16)
            found = found + dot_nn(pair, hit)
        slots_ref[q : q + 1] = (found[0:1] * 256.0 + found[1:2]).astype(I32)


def prepare(pos, codes, buckets, location, candidates, block):
    passages, height, width = codes.shape
    return pl.pallas_call(
        prepare_kernel,
        out_shape=(
            jax.ShapeDtypeStruct((passages + 8, height), I32),
            jax.ShapeDtypeStruct((passages, block, width), F32),
            jax.ShapeDtypeStruct(candidates.shape, I32),
        ),
        in_specs=[VMEM] * 5,
        out_specs=(VMEM, VMEM, VMEM),
        scratch_shapes=[
            pltpu.VMEM((passages + 8, height), I32),
            pltpu.SMEM(((passages + 1) * height,), I32),
            pltpu.VMEM((block + UNROLL, width), I32),
            pltpu.SemaphoreType.DMA((passages + 1,)),
        ],
        compiler_params=pltpu.CompilerParams(vmem_limit_bytes=56 * MIB),
    )(pos, codes, buckets, location, candidates)


def fetch_kernel(
    span, cap, received_hbm, table_hbm, after_ref, out_hbm,
    front, back, message, ask, asked, even, odd, out_ref, load_sems, out_sems, sems, sem,
):
    shards, _, height = received_hbm.shape
    half_tiles, _, width = front.shape
    per = list_rows(cap, height)
    rows = shards * per
    receive = pltpu.make_async_copy(
        received_hbm.at[:, pl.ds(span, message.shape[1])], message, sem
    )
    receive.start()
    loads = [
        pltpu.make_async_copy(table_hbm.at[pl.ds(h * half_tiles, half_tiles)], table, load_sems.at[h])
        for h, table in enumerate((front, back))
    ]
    loads[0].start()
    receive.wait()
    lane = lax.broadcasted_iota(I32, (1, height), 1)
    sizes = jnp.zeros((1, height), F32)
    for d in range(shards):
        lists = message[d].astype(F32)
        sizes = jnp.where(lane == d, lists[2 * per : 2 * per + 1], sizes)
        sizes = jnp.where(lane == d + shards, lists[2 * per + 1 : 2 * per + 2], sizes)
        offset = (lists[:per] * 256.0 + lists[per : 2 * per]).astype(I32)
        ask[d * per : (d + 1) * per] = (offset // TILE) & (half_tiles - 1)
        ask[rows + d * per : rows + (d + 1) * per] = offset & (TILE - 1)
    ask[2 * rows : 2 * rows + 1] = sizes.astype(I32)
    loads[1].start()
    copies = [
        pltpu.make_async_copy(ask.at[r], asked.at[pl.ds(r * height, height)], sems.at[r])
        for r in range(2 * rows + 1)
    ]
    for copy in copies:
        copy.start()
    for copy in copies:
        copy.wait()
    line = lax.broadcasted_iota(I32, (8, width), 0)

    def leave(d):
        own = pl.ds(pl.multiple_of(d * cap, cap), cap)
        return pltpu.make_async_copy(out_ref.at[own], out_hbm.at[own], out_sems.at[d])

    for h, table in enumerate((front, back)):
        loads[h].wait()

        @pl.loop(0, shards)
        def _(d):
            base = d * (per * height)
            count = asked[2 * rows * height + d]
            first = asked[2 * rows * height + shards + d]
            begin = 0 if h == 0 else first // TILE
            end = ((first if h == 0 else count) + TILE - 1) // TILE

            @pl.loop(begin, end)
            def _(i):
                at = pl.multiple_of(base + i * TILE, TILE)
                low_at = pl.multiple_of(at + rows * height, TILE)
                to = pl.multiple_of(d * cap + i * TILE, TILE)
                stages = (even, odd)
                for g, stage in enumerate(stages):
                    for u in range(8):
                        stage[u * TILE : (u + 1) * TILE] = table[asked[at + 8 * g + u]].astype(F32)
                if h == 0:
                    halves = [jnp.zeros((8, width), F32)] * 2
                else:
                    old = out_ref[pl.ds(to, TILE)].astype(F32)
                    halves = [old[:8], old[8:]]
                for g, stage in enumerate(stages):
                    for u in range(8):
                        row = stage[pl.ds(u * TILE + asked[low_at + 8 * g + u], 1)]
                        here = line == u
                        if h == 1:
                            here = here & (line + (i * TILE + 8 * g) >= first)
                        halves[g] = jnp.where(here, row, halves[g])
                out_ref[pl.ds(to, TILE)] = jnp.concatenate(halves, axis=0).astype(BF16)

            if h == 1:
                leave(d).start()

    for d in range(shards):
        leave(d).wait()


def fetch(received, table, after, span, cap):
    shard_rows, width = table.shape
    shards, length, height = received.shape
    rows = shards * list_rows(cap, height)
    assert shard_rows & (shard_rows - 1) == 0
    half = (shard_rows // TILE // 2, TILE, width)
    ask_rows = (2 * rows + 8) // 8 * 8
    return pl.pallas_call(
        functools.partial(fetch_kernel, span, cap),
        out_shape=jax.ShapeDtypeStruct((shards * cap, width), BF16),
        in_specs=[HBM, HBM, HBM],
        out_specs=HBM,
        scratch_shapes=[
            pltpu.VMEM(half, table.dtype),
            pltpu.VMEM(half, table.dtype),
            pltpu.VMEM((shards, length - span, height), BF16),
            pltpu.VMEM((ask_rows, height), I32),
            pltpu.SMEM((ask_rows * height,), I32),
            pltpu.VMEM((8 * TILE, width), F32),
            pltpu.VMEM((8 * TILE, width), F32),
            pltpu.VMEM((shards * cap, width), BF16),
            pltpu.SemaphoreType.DMA((2,)),
            pltpu.SemaphoreType.DMA((shards,)),
            pltpu.SemaphoreType.DMA((2 * rows + 1,)),
            pltpu.SemaphoreType.DMA,
        ],
        compiler_params=pltpu.CompilerParams(vmem_limit_bytes=56 * MIB),
    )(received, table.reshape(shard_rows // TILE, TILE, width), after)


def score_kernel(span, list_hbm, replies_ref, residual_hbm, *refs):
    passages, block, width = residual_hbm.shape
    *query_refs, out_ref, wide, tile, embedded, residual_ref, list_ref, sems = refs
    listing = pltpu.make_async_copy(list_hbm, list_ref, sems.at[0])
    listing.start()
    load = pltpu.make_async_copy(residual_hbm, residual_ref, sems.at[1])
    load.start()
    groups, subs = lax.axis_size("groups"), lax.axis_size("sub")
    own_group, own_sub = lax.axis_index("groups"), lax.axis_index("sub")
    shards = query_refs[0].shape[0]
    height = list_ref.shape[0] // (passages + 8)
    pair = 2 if shards % 2 == 0 else 1
    ahead = 4 if shards % (4 * pair) == 0 else 1

    @pl.loop(0, replies_ref.shape[0] // 256)
    def _(i):
        at = pl.multiple_of(i * 256, 256)
        wide[pl.ds(at, 256)] = replies_ref[pl.ds(at, 256)].astype(F32)

    listing.wait()

    @pl.loop(0, passages)
    def _(p):
        count = list_ref[passages * height + p]

        def move(at, rows):
            for u in range(rows):
                place = list_ref[p * height + at + u]
                tile[pl.ds(p * block + at + u, 1)] = wide[pl.ds(place, 1)]

        move(0, 32)

        @pl.loop(2, (count + UNROLL - 1) // UNROLL)
        def _(i):
            move(pl.multiple_of(i * UNROLL, UNROLL), UNROLL)

    load.wait()
    line = lax.broadcasted_iota(I32, (block, width), 0)
    here = lax.broadcasted_iota(I32, (passages, pair * span), 0)
    counts = jnp.zeros((passages, pair * span), I32)
    for p in range(0, passages, 2):
        both = []
        for q in (p, p + 1):
            count = list_ref[passages * height + q]
            counts = jnp.where(here == q, count, counts)
            rows = tile[q * block : (q + 1) * block] + residual_ref[q]
            both.append(jnp.where(line < count, rows, rows[0:1]))
        embedded[p * block : (p + 2) * block] = jnp.concatenate(both, axis=0).astype(BF16)

    for step, query_ref in enumerate(query_refs):
        group = lax.rem(own_group + groups - step // subs, groups)
        sub = lax.rem(own_sub + subs - step % subs, subs)

        def columns(c):
            queries = jnp.concatenate(
                [query_ref[c * pair + e, :span] for e in range(pair)], axis=0
            )
            scores = dot_nt(embedded[...], queries)
            best = jnp.max(scores.reshape(passages, block, pair * span), axis=1)
            best = jnp.where(counts > 0, best, -3e38)
            for e in range(pair):
                device = (group * shards + c * pair + e) * subs + sub
                out_ref[device] = best[:, e * span : (e + 1) * span]

        if shards == pair * ahead:
            for c in range(ahead):
                columns(c)
        else:

            @pl.loop(0, shards // (pair * ahead))
            def _(i):
                for h in range(ahead):
                    columns(i * ahead + h)


def score(lists, replies, residuals, queries, span):
    passages, block, width = residuals.shape
    devices = len(queries) * queries[0].shape[0]
    return pl.pallas_call(
        functools.partial(score_kernel, span),
        out_shape=jax.ShapeDtypeStruct((devices, passages, span), F32),
        in_specs=[HBM, VMEM, HBM] + [VMEM] * len(queries),
        out_specs=VMEM,
        scratch_shapes=[
            pltpu.VMEM((replies.shape[0], width), F32),
            pltpu.VMEM((passages * block + UNROLL, width), F32),
            pltpu.VMEM((passages * block, width), BF16),
            pltpu.VMEM((passages, block, width), F32),
            pltpu.SMEM(lists.shape, I32),
            pltpu.SemaphoreType.DMA((2,)),
        ],
        compiler_params=pltpu.CompilerParams(vmem_limit_bytes=24 * MIB),
    )(lists, replies, residuals, *queries)


def pick_kernel(tokens, slots_ref, best_ref, out_ref):
    owned, listed = slots_ref.shape
    parts, slots_total, span = best_ref.shape
    slot = lax.broadcasted_iota(I32, (slots_total, listed), 0)
    sums = best_ref[0]
    for g in range(1, parts):
        sums = jnp.maximum(sums, best_ref[g])
    shift = tokens // 2
    while shift:
        sums = sums + pltpu.roll(sums, span - shift, 1)
        shift //= 2
    for q in range(owned):
        column = jnp.broadcast_to(sums[:, q * tokens : q * tokens + 1], (slots_total, listed))
        chosen = jnp.where(slot == slots_ref[q : q + 1], column, 0.0)
        out_ref[q : q + 1] = jnp.sum(chosen, axis=0, keepdims=True)


def pick(slots, best, tokens):
    return pl.pallas_call(
        functools.partial(pick_kernel, tokens),
        out_shape=jax.ShapeDtypeStruct(slots.shape, F32),
        compiler_params=pltpu.CompilerParams(vmem_limit_bytes=16 * MIB),
    )(slots, best)


def turned(array, axis, shift):
    size = lax.axis_size(axis)
    return lax.ppermute(array, axis, [(i, (i + shift) % size) for i in range(size)])


def body(queries, candidates, location, lengths, centroid_ids, residual_codes, centroids, buckets):
    token_count = centroid_ids.shape[0]
    passages = lengths.shape[0]
    height = token_count // passages
    width = residual_codes.shape[1]
    shard_rows = centroids.shape[0]
    shards, subs, parts = lax.axis_size("blk"), lax.axis_size("sub"), lax.axis_size("groups")
    cap = 2 * token_count // shards // parts
    owned, tokens = queries.shape[0], queries.shape[1]
    span = owned * tokens

    sent, pos = plan(
        lengths,
        centroid_ids.reshape(passages, height),
        queries.reshape(span, width),
        shards,
        shard_rows,
        cap,
        parts,
    )
    near = lax.all_to_all(sent, "blk", split_axis=0, concat_axis=0, tiled=True)
    lists, residuals, slots = prepare(
        pos,
        residual_codes.reshape(passages, height, width),
        buckets,
        location.reshape(location.shape[0] // 128, 128),
        candidates,
        block_rows(height, shards, parts),
    )
    found = fetch(near, centroids, slots, span, cap)
    replies = lax.all_to_all(
        found.reshape(shards, cap, width), "blk", split_axis=0, concat_axis=0, tiled=True
    )
    across = [near] + [turned(near, "groups", g) for g in range(1, parts)]
    spread = []
    for array in across:
        others = [turned(array, "sub", s) for s in range(1, subs)]
        own = turned(others[-1], "sub", 1) if array is near and others else array
        spread += [own] + others
    best = score(lists.reshape(lists.size), replies.reshape(shards * cap, width), residuals, spread, span)
    mine = lax.all_to_all(best, ("groups", "blk", "sub"), split_axis=0, concat_axis=0, tiled=True)
    return pick(slots, mine.reshape(parts, shards * subs * passages, span), tokens)


def solution(mesh):
    in_specs = (
        P(("groups", "blk", "sub"), None, None),
        P(("groups", "blk", "sub"), None),
        P(),
        P(("blk", "sub")),
        P(("blk", "sub")),
        P(("blk", "sub"), None),
        P("blk", None),
        P(),
    )
    out_specs = P(("groups", "blk", "sub"), None)
    return jax.shard_map(body, mesh=mesh, in_specs=in_specs, out_specs=out_specs, check_vma=False)
```

```python
import functools

import jax
import jax.numpy as jnp
from jax import lax
from jax.experimental import pallas as pl
from jax.experimental.pallas import tpu as pltpu
from jax.sharding import PartitionSpec as P

F32 = jnp.float32
BF16 = jnp.bfloat16
I32 = jnp.int32
MIB = 1 << 20
UNROLL = 16
TILE = 16
SMEM = pl.BlockSpec(memory_space=pltpu.SMEM)
VMEM = pl.BlockSpec(memory_space=pltpu.VMEM)
HBM = pl.BlockSpec(memory_space=pl.ANY)


def dot_nt(a, b):
    return lax.dot_general(a, b, (((1,), (1,)), ((), ())), preferred_element_type=F32)


def dot_nn(a, b):
    return lax.dot_general(a, b, (((1,), (0,)), ((), ())), preferred_element_type=F32)


def plan_kernel(
    shards, shard_rows, cap, parts, lengths_hbm, ids_hbm, queries_hbm, sent_ref, pos_ref,
    lengths_ref, ids_ref, queries_ref, sems,
):
    copies = [
        pltpu.make_async_copy(lengths_hbm, lengths_ref, sems.at[0]),
        pltpu.make_async_copy(ids_hbm, ids_ref, sems.at[1]),
        pltpu.make_async_copy(queries_hbm, queries_ref, sems.at[2]),
    ]
    for copy in copies:
        copy.start()
    for copy in copies[:2]:
        copy.wait()
    passages, height = ids_ref.shape
    span = queries_ref.shape[0]
    part = lax.axis_index("groups")
    ids = ids_ref[...]
    owner = ids // shard_rows
    offset = ids - owner * shard_rows
    row = lax.broadcasted_iota(I32, (passages, height), 0)
    lane = lax.broadcasted_iota(I32, (passages, height), 1)
    limit = jnp.zeros((passages, height), I32)
    for p in range(passages):
        limit = jnp.where(row == p, lengths_ref[p], limit)
    owner = jnp.where(lane < limit, owner, shards)
    kind = 2 * owner + offset // (shard_rows // 2)
    kinds = 2 * shards
    mask = jnp.concatenate([jnp.where(kind == b, 1.0, 0.0) for b in range(kinds)], axis=0)
    mask16 = mask.astype(BF16)
    k = lax.broadcasted_iota(I32, (height, height), 0)
    l = lax.broadcasted_iota(I32, (height, height), 1)
    inside = dot_nn(mask16, jnp.where(k < l, 1.0, 0.0).astype(BF16))
    totals = dot_nn(mask16, jnp.ones((height, height), BF16))
    full = kinds * passages
    r = lax.broadcasted_iota(I32, (full, full), 0)
    c = lax.broadcasted_iota(I32, (full, full), 1)
    same = r // (2 * passages) == c // (2 * passages)
    ahead = dot_nn(jnp.where(same & (c < r), 1.0, 0.0).astype(BF16), totals.astype(BF16))
    place = (inside + ahead) * mask
    rank = jnp.zeros((passages, height), F32)
    sizes = []
    for b in range(kinds):
        rank = rank + place[b * passages : (b + 1) * passages]
        size = jnp.sum(totals[b * passages : (b + 1) * passages], axis=0, keepdims=True)
        sizes.append(size.astype(I32))
    rank = rank.astype(I32)
    mine = (lane < limit) & (rank % parts == part)
    rank = rank // parts
    pos_ref[...] = jnp.where(mine, owner * cap + rank, -1)
    per = list_rows(cap, height)
    list_row = jnp.where(mine, owner * per + rank // height, -1)
    list_lane = rank % height
    high = (offset // 256).astype(F32)
    low = (offset % 256).astype(F32)
    rows = shards * per
    out_row = lax.broadcasted_iota(I32, (rows, height), 0)
    at_lane = lax.broadcasted_iota(I32, (height, height), 0)
    sums = jnp.zeros((rows, 2 * height), F32)
    for p in range(passages):
        here = jnp.where(out_row == list_row[p : p + 1], 1.0, 0.0).astype(BF16)
        hit = at_lane == list_lane[p : p + 1]
        values = jnp.concatenate(
            [jnp.where(hit, high[p : p + 1], 0.0), jnp.where(hit, low[p : p + 1], 0.0)], axis=0
        ).astype(BF16)
        sums = sums + dot_nt(here, values)
    copies[2].wait()
    queries = queries_ref[...]
    extra = message_rows(cap, height)
    for b in range(shards):
        share = (sizes[2 * b] + sizes[2 * b + 1] + (parts - 1 - part)) // parts
        first = (sizes[2 * b] + (parts - 1 - part)) // parts
        sent_ref[b, :span] = queries
        sent_ref[b, span:] = jnp.concatenate(
            [
                sums[b * per : (b + 1) * per, :height],
                sums[b * per : (b + 1) * per, height:],
                share.astype(F32),
                first.astype(F32),
                jnp.zeros((extra - 2 * per - 2, height), F32),
            ],
            axis=0,
        ).astype(BF16)


def list_rows(cap, lanes):
    return (cap + lanes - 1) // lanes


def message_rows(cap, lanes):
    return (2 * list_rows(cap, lanes) + 1 + TILE) // TILE * TILE


def plan(lengths, ids, queries, shards, shard_rows, cap, parts):
    passages, height = ids.shape
    span = queries.shape[0]
    return pl.pallas_call(
        functools.partial(plan_kernel, shards, shard_rows, cap, parts),
        out_shape=(
            jax.ShapeDtypeStruct((shards, span + message_rows(cap, height), height), BF16),
            jax.ShapeDtypeStruct((passages, height), I32),
        ),
        in_specs=[HBM, HBM, HBM],
        out_specs=(VMEM, VMEM),
        scratch_shapes=[
            pltpu.SMEM(lengths.shape, I32),
            pltpu.VMEM(ids.shape, I32),
            pltpu.VMEM(queries.shape, BF16),
            pltpu.SemaphoreType.DMA((3,)),
        ],
        compiler_params=pltpu.CompilerParams(vmem_limit_bytes=56 * MIB),
    )(lengths, ids, queries)


def block_rows(height, shards, parts):
    most = min(height, (height + 2 * shards * (parts - 1)) // parts)
    return (most + 7) // 8 * 8


def prepare_kernel(
    pos_ref, codes_ref, buckets_ref, location_ref, candidates_ref,
    list_ref, residual_ref, slots_ref, tokens, flat, picked, sems,
):
    passages, height = pos_ref.shape
    block, width = residual_ref.shape[1:]
    pos = pos_ref[...]
    mine = jnp.where(pos >= 0, 1.0, 0.0).astype(BF16)
    k = lax.broadcasted_iota(I32, (height, height), 0)
    l = lax.broadcasted_iota(I32, (height, height), 1)
    rank = dot_nn(mine, jnp.where(k < l, 1.0, 0.0).astype(BF16))
    total = dot_nn(mine, jnp.ones((height, height), BF16)).astype(I32)
    rank = jnp.where(pos >= 0, rank.astype(I32), -1)
    high = (pos // 256).astype(F32)
    low = (pos % 256).astype(F32)
    token = lax.broadcasted_iota(I32, (1, height), 1).astype(F32)
    lane = lax.broadcasted_iota(I32, (1, height), 1)
    counts = jnp.zeros((1, height), I32)
    for p in range(passages):
        hit = jnp.where(k == rank[p : p + 1], 1.0, 0.0).astype(BF16)
        values = jnp.concatenate([high[p : p + 1], low[p : p + 1], token], axis=0).astype(BF16)
        found = dot_nt(values, hit).astype(I32)
        list_ref[p : p + 1] = found[0:1] * 256 + found[1:2]
        tokens[p : p + 1] = found[2:3]
        counts = jnp.where(lane == p, total[p : p + 1], counts)
    list_ref[passages : passages + 1] = counts
    tokens[passages : passages + 1] = counts
    copies = [
        pltpu.make_async_copy(tokens.at[p], flat.at[pl.ds(p * height, height)], sems.at[p])
        for p in range(passages + 1)
    ]
    for copy in copies:
        copy.start()
    for copy in copies:
        copy.wait()

    @pl.loop(0, passages)
    def _(p):
        count = flat[passages * height + p]

        @pl.loop(0, (count + UNROLL - 1) // UNROLL)
        def _(i):
            at = pl.multiple_of(i * UNROLL, UNROLL)
            for u in range(UNROLL):
                picked[pl.ds(at + u, 1)] = codes_ref[p, pl.ds(flat[p * height + at + u], 1)]

        codes = picked[:block]
        residual_ref[p] = jnp.where(
            codes == 0,
            buckets_ref[0:1],
            jnp.where(
                codes == 1,
                buckets_ref[1:2],
                jnp.where(codes == 2, buckets_ref[2:3], buckets_ref[3:4]),
            ),
        )

    owned, listed = candidates_ref.shape
    blocks, width = location_ref.shape
    which = lax.broadcasted_iota(I32, (width, listed), 0)
    for q in range(owned):
        named = candidates_ref[q : q + 1]
        found = jnp.zeros((2, listed), F32)
        for g in range(blocks):
            here = location_ref[g : g + 1]
            pair = jnp.concatenate([here // 256, here % 256], axis=0).astype(F32).astype(BF16)
            hit = jnp.where(which + g * width == named, 1.0, 0.0).astype(BF16)
            found = found + dot_nn(pair, hit)
        slots_ref[q : q + 1] = (found[0:1] * 256.0 + found[1:2]).astype(I32)


def prepare(pos, codes, buckets, location, candidates, block):
    passages, height, width = codes.shape
    return pl.pallas_call(
        prepare_kernel,
        out_shape=(
            jax.ShapeDtypeStruct((passages + 8, height), I32),
            jax.ShapeDtypeStruct((passages, block, width), F32),
            jax.ShapeDtypeStruct(candidates.shape, I32),
        ),
        in_specs=[VMEM] * 5,
        out_specs=(VMEM, VMEM, VMEM),
        scratch_shapes=[
            pltpu.VMEM((passages + 8, height), I32),
            pltpu.SMEM(((passages + 1) * height,), I32),
            pltpu.VMEM((block + UNROLL, width), I32),
            pltpu.SemaphoreType.DMA((passages + 1,)),
        ],
        compiler_params=pltpu.CompilerParams(vmem_limit_bytes=56 * MIB),
    )(pos, codes, buckets, location, candidates)


def fetch_kernel(
    span, cap, received_hbm, table_hbm, after_ref, out_hbm,
    front, back, message, ask, asked, even, odd, out_ref, load_sems, out_sems, sems, sem,
):
    shards, _, height = received_hbm.shape
    half_tiles, _, width = front.shape
    per = list_rows(cap, height)
    rows = shards * per
    receive = pltpu.make_async_copy(
        received_hbm.at[:, pl.ds(span, message.shape[1])], message, sem
    )
    receive.start()
    loads = [
        pltpu.make_async_copy(table_hbm.at[pl.ds(h * half_tiles, half_tiles)], table, load_sems.at[h])
        for h, table in enumerate((front, back))
    ]
    loads[0].start()
    receive.wait()
    lane = lax.broadcasted_iota(I32, (1, height), 1)
    sizes = jnp.zeros((1, height), F32)
    for d in range(shards):
        lists = message[d].astype(F32)
        sizes = jnp.where(lane == d, lists[2 * per : 2 * per + 1], sizes)
        sizes = jnp.where(lane == d + shards, lists[2 * per + 1 : 2 * per + 2], sizes)
        offset = (lists[:per] * 256.0 + lists[per : 2 * per]).astype(I32)
        ask[d * per : (d + 1) * per] = (offset // TILE) & (half_tiles - 1)
        ask[rows + d * per : rows + (d + 1) * per] = offset & (TILE - 1)
    ask[2 * rows : 2 * rows + 1] = sizes.astype(I32)
    loads[1].start()
    copies = [
        pltpu.make_async_copy(ask.at[r], asked.at[pl.ds(r * height, height)], sems.at[r])
        for r in range(2 * rows + 1)
    ]
    for copy in copies:
        copy.start()
    for copy in copies:
        copy.wait()
    line = lax.broadcasted_iota(I32, (8, width), 0)

    def leave(d):
        own = pl.ds(pl.multiple_of(d * cap, cap), cap)
        return pltpu.make_async_copy(out_ref.at[own], out_hbm.at[own], out_sems.at[d])

    for h, table in enumerate((front, back)):
        loads[h].wait()

        @pl.loop(0, shards, unroll=4)
        def _(d):
            base = d * (per * height)
            count = asked[2 * rows * height + d]
            first = asked[2 * rows * height + shards + d]
            begin = 0 if h == 0 else first // TILE
            end = ((first if h == 0 else count) + TILE - 1) // TILE

            @pl.loop(begin, end)
            def _(i):
                at = pl.multiple_of(base + i * TILE, TILE)
                low_at = pl.multiple_of(at + rows * height, TILE)
                to = pl.multiple_of(d * cap + i * TILE, TILE)
                stages = (even, odd)
                for g, stage in enumerate(stages):
                    for u in range(8):
                        stage[u * TILE : (u + 1) * TILE] = table[asked[at + 8 * g + u]].astype(F32)
                if h == 0:
                    halves = [jnp.zeros((8, width), F32)] * 2
                else:
                    old = out_ref[pl.ds(to, TILE)].astype(F32)
                    halves = [old[:8], old[8:]]
                for g, stage in enumerate(stages):
                    for u in range(8):
                        row = stage[pl.ds(u * TILE + asked[low_at + 8 * g + u], 1)]
                        here = line == u
                        if h == 1:
                            here = here & (line + (i * TILE + 8 * g) >= first)
                        halves[g] = jnp.where(here, row, halves[g])
                out_ref[pl.ds(to, TILE)] = jnp.concatenate(halves, axis=0).astype(BF16)

            if h == 1:
                leave(d).start()

    for d in range(shards):
        leave(d).wait()


def fetch(received, table, after, span, cap):
    shard_rows, width = table.shape
    shards, length, height = received.shape
    rows = shards * list_rows(cap, height)
    assert shard_rows & (shard_rows - 1) == 0
    half = (shard_rows // TILE // 2, TILE, width)
    ask_rows = (2 * rows + 8) // 8 * 8
    return pl.pallas_call(
        functools.partial(fetch_kernel, span, cap),
        out_shape=jax.ShapeDtypeStruct((shards * cap, width), BF16),
        in_specs=[HBM, HBM, HBM],
        out_specs=HBM,
        scratch_shapes=[
            pltpu.VMEM(half, table.dtype),
            pltpu.VMEM(half, table.dtype),
            pltpu.VMEM((shards, length - span, height), BF16),
            pltpu.VMEM((ask_rows, height), I32),
            pltpu.SMEM((ask_rows * height,), I32),
            pltpu.VMEM((8 * TILE, width), F32),
            pltpu.VMEM((8 * TILE, width), F32),
            pltpu.VMEM((shards * cap, width), BF16),
            pltpu.SemaphoreType.DMA((2,)),
            pltpu.SemaphoreType.DMA((shards,)),
            pltpu.SemaphoreType.DMA((2 * rows + 1,)),
            pltpu.SemaphoreType.DMA,
        ],
        compiler_params=pltpu.CompilerParams(vmem_limit_bytes=56 * MIB),
    )(received, table.reshape(shard_rows // TILE, TILE, width), after)


def score_kernel(span, list_hbm, replies_ref, residual_hbm, *refs):
    passages, block, width = residual_hbm.shape
    *query_refs, out_ref, wide, tile, embedded, residual_ref, list_ref, sems = refs
    listing = pltpu.make_async_copy(list_hbm, list_ref, sems.at[0])
    listing.start()
    load = pltpu.make_async_copy(residual_hbm, residual_ref, sems.at[1])
    load.start()
    groups, subs = lax.axis_size("groups"), lax.axis_size("sub")
    own_group, own_sub = lax.axis_index("groups"), lax.axis_index("sub")
    shards = query_refs[0].shape[0]
    height = list_ref.shape[0] // (passages + 8)
    pair = 2 if shards % 2 == 0 else 1
    ahead = 4 if shards % (4 * pair) == 0 else 1

    @pl.loop(0, replies_ref.shape[0] // 256)
    def _(i):
        at = pl.multiple_of(i * 256, 256)
        wide[pl.ds(at, 256)] = replies_ref[pl.ds(at, 256)].astype(F32)

    listing.wait()

    @pl.loop(0, passages)
    def _(p):
        count = list_ref[passages * height + p]

        def move(at, rows):
            for u in range(rows):
                place = list_ref[p * height + at + u]
                tile[pl.ds(p * block + at + u, 1)] = wide[pl.ds(place, 1)]

        move(0, 32)

        @pl.loop(2, (count + UNROLL - 1) // UNROLL)
        def _(i):
            move(pl.multiple_of(i * UNROLL, UNROLL), UNROLL)

    load.wait()
    line = lax.broadcasted_iota(I32, (block, width), 0)
    here = lax.broadcasted_iota(I32, (passages, pair * span), 0)
    counts = jnp.zeros((passages, pair * span), I32)
    for p in range(0, passages, 2):
        both = []
        for q in (p, p + 1):
            count = list_ref[passages * height + q]
            counts = jnp.where(here == q, count, counts)
            rows = tile[q * block : (q + 1) * block] + residual_ref[q]
            both.append(jnp.where(line < count, rows, rows[0:1]))
        embedded[p * block : (p + 2) * block] = jnp.concatenate(both, axis=0).astype(BF16)

    for step, query_ref in enumerate(query_refs):
        group = lax.rem(own_group + groups - step // subs, groups)
        sub = lax.rem(own_sub + subs - step % subs, subs)

        def columns(c):
            queries = jnp.concatenate(
                [query_ref[c * pair + e, :span] for e in range(pair)], axis=0
            )
            scores = dot_nt(embedded[...], queries)
            best = jnp.max(scores.reshape(passages, block, pair * span), axis=1)
            best = jnp.where(counts > 0, best, -3e38)
            for e in range(pair):
                device = (group * shards + c * pair + e) * subs + sub
                out_ref[device] = best[:, e * span : (e + 1) * span]

        if shards == pair * ahead:
            for c in range(ahead):
                columns(c)
        else:

            @pl.loop(0, shards // (pair * ahead))
            def _(i):
                for h in range(ahead):
                    columns(i * ahead + h)


def score(lists, replies, residuals, queries, span):
    passages, block, width = residuals.shape
    devices = len(queries) * queries[0].shape[0]
    return pl.pallas_call(
        functools.partial(score_kernel, span),
        out_shape=jax.ShapeDtypeStruct((devices, passages, span), F32),
        in_specs=[HBM, VMEM, HBM] + [VMEM] * len(queries),
        out_specs=VMEM,
        scratch_shapes=[
            pltpu.VMEM((replies.shape[0], width), F32),
            pltpu.VMEM((passages * block + UNROLL, width), F32),
            pltpu.VMEM((passages * block, width), BF16),
            pltpu.VMEM((passages, block, width), F32),
            pltpu.SMEM(lists.shape, I32),
            pltpu.SemaphoreType.DMA((2,)),
        ],
        compiler_params=pltpu.CompilerParams(vmem_limit_bytes=24 * MIB),
    )(lists, replies, residuals, *queries)


def pick_kernel(tokens, slots_ref, best_ref, out_ref):
    owned, listed = slots_ref.shape
    parts, slots_total, span = best_ref.shape
    slot = lax.broadcasted_iota(I32, (slots_total, listed), 0)
    sums = best_ref[0]
    for g in range(1, parts):
        sums = jnp.maximum(sums, best_ref[g])
    shift = tokens // 2
    while shift:
        sums = sums + pltpu.roll(sums, span - shift, 1)
        shift //= 2
    for q in range(owned):
        column = jnp.broadcast_to(sums[:, q * tokens : q * tokens + 1], (slots_total, listed))
        chosen = jnp.where(slot == slots_ref[q : q + 1], column, 0.0)
        out_ref[q : q + 1] = jnp.sum(chosen, axis=0, keepdims=True)


def pick(slots, best, tokens):
    return pl.pallas_call(
        functools.partial(pick_kernel, tokens),
        out_shape=jax.ShapeDtypeStruct(slots.shape, F32),
        compiler_params=pltpu.CompilerParams(vmem_limit_bytes=16 * MIB),
    )(slots, best)


def turned(array, axis, shift):
    size = lax.axis_size(axis)
    return lax.ppermute(array, axis, [(i, (i + shift) % size) for i in range(size)])


def body(queries, candidates, location, lengths, centroid_ids, residual_codes, centroids, buckets):
    token_count = centroid_ids.shape[0]
    passages = lengths.shape[0]
    height = token_count // passages
    width = residual_codes.shape[1]
    shard_rows = centroids.shape[0]
    shards, subs, parts = lax.axis_size("blk"), lax.axis_size("sub"), lax.axis_size("groups")
    cap = 2 * token_count // shards // parts
    owned, tokens = queries.shape[0], queries.shape[1]
    span = owned * tokens

    sent, pos = plan(
        lengths,
        centroid_ids.reshape(passages, height),
        queries.reshape(span, width),
        shards,
        shard_rows,
        cap,
        parts,
    )
    near = lax.all_to_all(sent, "blk", split_axis=0, concat_axis=0, tiled=True)
    lists, residuals, slots = prepare(
        pos,
        residual_codes.reshape(passages, height, width),
        buckets,
        location.reshape(location.shape[0] // 128, 128),
        candidates,
        block_rows(height, shards, parts),
    )
    found = fetch(near, centroids, slots, span, cap)
    replies = lax.all_to_all(
        found.reshape(shards, cap, width), "blk", split_axis=0, concat_axis=0, tiled=True
    )
    across = [near] + [turned(near, "groups", g) for g in range(1, parts)]
    spread = []
    for array in across:
        others = [turned(array, "sub", s) for s in range(1, subs)]
        own = turned(others[-1], "sub", 1) if array is near and others else array
        spread += [own] + others
    best = score(lists.reshape(lists.size), replies.reshape(shards * cap, width), residuals, spread, span)
    mine = lax.all_to_all(best, ("groups", "blk", "sub"), split_axis=0, concat_axis=0, tiled=True)
    return pick(slots, mine.reshape(parts, shards * subs * passages, span), tokens)


def solution(mesh):
    in_specs = (
        P(("groups", "blk", "sub"), None, None),
        P(("groups", "blk", "sub"), None),
        P(),
        P(("blk", "sub")),
        P(("blk", "sub")),
        P(("blk", "sub"), None),
        P("blk", None),
        P(),
    )
    out_specs = P(("groups", "blk", "sub"), None)
    return jax.shard_map(body, mesh=mesh, in_specs=in_specs, out_specs=out_specs, check_vma=False)
```

```python
import functools

import jax
import jax.numpy as jnp
from jax import lax
from jax.experimental import pallas as pl
from jax.experimental.pallas import tpu as pltpu
from jax.sharding import PartitionSpec as P

F32 = jnp.float32
BF16 = jnp.bfloat16
I32 = jnp.int32
MIB = 1 << 20
UNROLL = 16
TILE = 16
SMEM = pl.BlockSpec(memory_space=pltpu.SMEM)
VMEM = pl.BlockSpec(memory_space=pltpu.VMEM)
HBM = pl.BlockSpec(memory_space=pl.ANY)


def dot_nt(a, b):
    return lax.dot_general(a, b, (((1,), (1,)), ((), ())), preferred_element_type=F32)


def dot_nn(a, b):
    return lax.dot_general(a, b, (((1,), (0,)), ((), ())), preferred_element_type=F32)


def plan_kernel(
    shards, shard_rows, cap, parts, lengths_hbm, ids_hbm, queries_hbm, sent_ref, pos_ref,
    lengths_ref, ids_ref, queries_ref, sems,
):
    copies = [
        pltpu.make_async_copy(lengths_hbm, lengths_ref, sems.at[0]),
        pltpu.make_async_copy(ids_hbm, ids_ref, sems.at[1]),
        pltpu.make_async_copy(queries_hbm, queries_ref, sems.at[2]),
    ]
    for copy in copies:
        copy.start()
    for copy in copies[:2]:
        copy.wait()
    passages, height = ids_ref.shape
    span = queries_ref.shape[0]
    part = lax.axis_index("groups")
    ids = ids_ref[...]
    owner = ids // shard_rows
    offset = ids - owner * shard_rows
    row = lax.broadcasted_iota(I32, (passages, height), 0)
    lane = lax.broadcasted_iota(I32, (passages, height), 1)
    limit = jnp.zeros((passages, height), I32)
    for p in range(passages):
        limit = jnp.where(row == p, lengths_ref[p], limit)
    owner = jnp.where(lane < limit, owner, shards)
    kind = 2 * owner + offset // (shard_rows // 2)
    kinds = 2 * shards
    mask = jnp.concatenate([jnp.where(kind == b, 1.0, 0.0) for b in range(kinds)], axis=0)
    mask16 = mask.astype(BF16)
    k = lax.broadcasted_iota(I32, (height, height), 0)
    l = lax.broadcasted_iota(I32, (height, height), 1)
    inside = dot_nn(mask16, jnp.where(k < l, 1.0, 0.0).astype(BF16))
    totals = dot_nn(mask16, jnp.ones((height, height), BF16))
    full = kinds * passages
    r = lax.broadcasted_iota(I32, (full, full), 0)
    c = lax.broadcasted_iota(I32, (full, full), 1)
    same = r // (2 * passages) == c // (2 * passages)
    ahead = dot_nn(jnp.where(same & (c < r), 1.0, 0.0).astype(BF16), totals.astype(BF16))
    place = (inside + ahead) * mask
    rank = jnp.zeros((passages, height), F32)
    sizes = []
    for b in range(kinds):
        rank = rank + place[b * passages : (b + 1) * passages]
        size = jnp.sum(totals[b * passages : (b + 1) * passages], axis=0, keepdims=True)
        sizes.append(size.astype(I32))
    rank = rank.astype(I32)
    mine = (lane < limit) & (rank % parts == part)
    rank = rank // parts
    pos_ref[...] = jnp.where(mine, owner * cap + rank, -1)
    per = list_rows(cap, height)
    list_row = jnp.where(mine, owner * per + rank // height, -1)
    list_lane = rank % height
    high = (offset // 256).astype(F32)
    low = (offset % 256).astype(F32)
    rows = shards * per
    out_row = lax.broadcasted_iota(I32, (rows, height), 0)
    at_lane = lax.broadcasted_iota(I32, (height, height), 0)
    sums = jnp.zeros((rows, 2 * height), F32)
    for p in range(passages):
        here = jnp.where(out_row == list_row[p : p + 1], 1.0, 0.0).astype(BF16)
        hit = at_lane == list_lane[p : p + 1]
        values = jnp.concatenate(
            [jnp.where(hit, high[p : p + 1], 0.0), jnp.where(hit, low[p : p + 1], 0.0)], axis=0
        ).astype(BF16)
        sums = sums + dot_nt(here, values)
    copies[2].wait()
    queries = queries_ref[...]
    extra = message_rows(cap, height)
    for b in range(shards):
        share = (sizes[2 * b] + sizes[2 * b + 1] + (parts - 1 - part)) // parts
        first = (sizes[2 * b] + (parts - 1 - part)) // parts
        sent_ref[b, :span] = queries
        sent_ref[b, span:] = jnp.concatenate(
            [
                sums[b * per : (b + 1) * per, :height],
                sums[b * per : (b + 1) * per, height:],
                share.astype(F32),
                first.astype(F32),
                jnp.zeros((extra - 2 * per - 2, height), F32),
            ],
            axis=0,
        ).astype(BF16)


def list_rows(cap, lanes):
    return (cap + lanes - 1) // lanes


def message_rows(cap, lanes):
    return (2 * list_rows(cap, lanes) + 1 + TILE) // TILE * TILE


def plan(lengths, ids, queries, shards, shard_rows, cap, parts):
    passages, height = ids.shape
    span = queries.shape[0]
    return pl.pallas_call(
        functools.partial(plan_kernel, shards, shard_rows, cap, parts),
        out_shape=(
            jax.ShapeDtypeStruct((shards, span + message_rows(cap, height), height), BF16),
            jax.ShapeDtypeStruct((passages, height), I32),
        ),
        in_specs=[HBM, HBM, HBM],
        out_specs=(VMEM, VMEM),
        scratch_shapes=[
            pltpu.SMEM(lengths.shape, I32),
            pltpu.VMEM(ids.shape, I32),
            pltpu.VMEM(queries.shape, BF16),
            pltpu.SemaphoreType.DMA((3,)),
        ],
        compiler_params=pltpu.CompilerParams(vmem_limit_bytes=56 * MIB),
    )(lengths, ids, queries)


def block_rows(height, shards, parts):
    most = min(height, (height + 2 * shards * (parts - 1)) // parts)
    return (most + 7) // 8 * 8


def prepare_kernel(
    pos_ref, codes_ref, buckets_ref, location_ref, candidates_ref,
    list_ref, residual_ref, slots_ref, tokens, flat, picked, sems,
):
    passages, height = pos_ref.shape
    block, width = residual_ref.shape[1:]
    pos = pos_ref[...]
    mine = jnp.where(pos >= 0, 1.0, 0.0).astype(BF16)
    k = lax.broadcasted_iota(I32, (height, height), 0)
    l = lax.broadcasted_iota(I32, (height, height), 1)
    rank = dot_nn(mine, jnp.where(k < l, 1.0, 0.0).astype(BF16))
    total = dot_nn(mine, jnp.ones((height, height), BF16)).astype(I32)
    rank = jnp.where(pos >= 0, rank.astype(I32), -1)
    high = (pos // 256).astype(F32)
    low = (pos % 256).astype(F32)
    token = lax.broadcasted_iota(I32, (1, height), 1).astype(F32)
    lane = lax.broadcasted_iota(I32, (1, height), 1)
    counts = jnp.zeros((1, height), I32)
    for p in range(passages):
        hit = jnp.where(k == rank[p : p + 1], 1.0, 0.0).astype(BF16)
        values = jnp.concatenate([high[p : p + 1], low[p : p + 1], token], axis=0).astype(BF16)
        found = dot_nt(values, hit).astype(I32)
        list_ref[p : p + 1] = found[0:1] * 256 + found[1:2]
        tokens[p : p + 1] = found[2:3]
        counts = jnp.where(lane == p, total[p : p + 1], counts)
    list_ref[passages : passages + 1] = counts
    tokens[passages : passages + 1] = counts
    copies = [
        pltpu.make_async_copy(tokens.at[p], flat.at[pl.ds(p * height, height)], sems.at[p])
        for p in range(passages + 1)
    ]
    for copy in copies:
        copy.start()
    for copy in copies:
        copy.wait()

    @pl.loop(0, passages)
    def _(p):
        count = flat[passages * height + p]

        @pl.loop(0, (count + UNROLL - 1) // UNROLL)
        def _(i):
            at = pl.multiple_of(i * UNROLL, UNROLL)
            for u in range(UNROLL):
                picked[pl.ds(at + u, 1)] = codes_ref[p, pl.ds(flat[p * height + at + u], 1)]

        codes = picked[:block]
        residual_ref[p] = jnp.where(
            codes == 0,
            buckets_ref[0:1],
            jnp.where(
                codes == 1,
                buckets_ref[1:2],
                jnp.where(codes == 2, buckets_ref[2:3], buckets_ref[3:4]),
            ),
        )

    owned, listed = candidates_ref.shape
    blocks, width = location_ref.shape
    which = lax.broadcasted_iota(I32, (width, listed), 0)
    for q in range(owned):
        named = candidates_ref[q : q + 1]
        found = jnp.zeros((2, listed), F32)
        for g in range(blocks):
            here = location_ref[g : g + 1]
            pair = jnp.concatenate([here // 256, here % 256], axis=0).astype(F32).astype(BF16)
            hit = jnp.where(which + g * width == named, 1.0, 0.0).astype(BF16)
            found = found + dot_nn(pair, hit)
        slots_ref[q : q + 1] = (found[0:1] * 256.0 + found[1:2]).astype(I32)


def prepare(pos, codes, buckets, location, candidates, block):
    passages, height, width = codes.shape
    return pl.pallas_call(
        prepare_kernel,
        out_shape=(
            jax.ShapeDtypeStruct((passages + 8, height), I32),
            jax.ShapeDtypeStruct((passages, block, width), F32),
            jax.ShapeDtypeStruct(candidates.shape, I32),
        ),
        in_specs=[VMEM] * 5,
        out_specs=(VMEM, VMEM, VMEM),
        scratch_shapes=[
            pltpu.VMEM((passages + 8, height), I32),
            pltpu.SMEM(((passages + 1) * height,), I32),
            pltpu.VMEM((block + UNROLL, width), I32),
            pltpu.SemaphoreType.DMA((passages + 1,)),
        ],
        compiler_params=pltpu.CompilerParams(vmem_limit_bytes=56 * MIB),
    )(pos, codes, buckets, location, candidates)


def fetch_kernel(
    span, cap, received_hbm, table_hbm, after_ref, out_hbm,
    front, back, message, ask, asked, even, odd, out_ref, load_sems, out_sems, sems, sem,
):
    shards, _, height = received_hbm.shape
    half_tiles, _, width = front.shape
    per = list_rows(cap, height)
    rows = shards * per
    receive = pltpu.make_async_copy(
        received_hbm.at[:, pl.ds(span, message.shape[1])], message, sem
    )
    receive.start()
    loads = [
        pltpu.make_async_copy(table_hbm.at[pl.ds(h * half_tiles, half_tiles)], table, load_sems.at[h])
        for h, table in enumerate((front, back))
    ]
    loads[0].start()
    receive.wait()
    lane = lax.broadcasted_iota(I32, (1, height), 1)
    sizes = jnp.zeros((1, height), F32)
    for d in range(shards):
        lists = message[d].astype(F32)
        sizes = jnp.where(lane == d, lists[2 * per : 2 * per + 1], sizes)
        sizes = jnp.where(lane == d + shards, lists[2 * per + 1 : 2 * per + 2], sizes)
        offset = (lists[:per] * 256.0 + lists[per : 2 * per]).astype(I32)
        ask[d * per : (d + 1) * per] = (offset // TILE) & (half_tiles - 1)
        ask[rows + d * per : rows + (d + 1) * per] = offset & (TILE - 1)
    ask[2 * rows : 2 * rows + 1] = sizes.astype(I32)
    loads[1].start()
    copies = [
        pltpu.make_async_copy(ask.at[r], asked.at[pl.ds(r * height, height)], sems.at[r])
        for r in range(2 * rows + 1)
    ]
    for copy in copies:
        copy.start()
    for copy in copies:
        copy.wait()
    line = lax.broadcasted_iota(I32, (8, width), 0)

    def leave(d):
        own = pl.ds(pl.multiple_of(d * cap, cap), cap)
        return pltpu.make_async_copy(out_ref.at[own], out_hbm.at[own], out_sems.at[d])

    for h, table in enumerate((front, back)):
        loads[h].wait()

        @pl.loop(0, shards, unroll=8)
        def _(d):
            base = d * (per * height)
            count = asked[2 * rows * height + d]
            first = asked[2 * rows * height + shards + d]
            begin = 0 if h == 0 else first // TILE
            end = ((first if h == 0 else count) + TILE - 1) // TILE

            @pl.loop(begin, end)
            def _(i):
                at = pl.multiple_of(base + i * TILE, TILE)
                low_at = pl.multiple_of(at + rows * height, TILE)
                to = pl.multiple_of(d * cap + i * TILE, TILE)
                stages = (even, odd)
                for g, stage in enumerate(stages):
                    for u in range(8):
                        stage[u * TILE : (u + 1) * TILE] = table[asked[at + 8 * g + u]].astype(F32)
                if h == 0:
                    halves = [jnp.zeros((8, width), F32)] * 2
                else:
                    old = out_ref[pl.ds(to, TILE)].astype(F32)
                    halves = [old[:8], old[8:]]
                for g, stage in enumerate(stages):
                    for u in range(8):
                        row = stage[pl.ds(u * TILE + asked[low_at + 8 * g + u], 1)]
                        here = line == u
                        if h == 1:
                            here = here & (line + (i * TILE + 8 * g) >= first)
                        halves[g] = jnp.where(here, row, halves[g])
                out_ref[pl.ds(to, TILE)] = jnp.concatenate(halves, axis=0).astype(BF16)

            if h == 1:
                leave(d).start()

    for d in range(shards):
        leave(d).wait()


def fetch(received, table, after, span, cap):
    shard_rows, width = table.shape
    shards, length, height = received.shape
    rows = shards * list_rows(cap, height)
    assert shard_rows & (shard_rows - 1) == 0
    half = (shard_rows // TILE // 2, TILE, width)
    ask_rows = (2 * rows + 8) // 8 * 8
    return pl.pallas_call(
        functools.partial(fetch_kernel, span, cap),
        out_shape=jax.ShapeDtypeStruct((shards * cap, width), BF16),
        in_specs=[HBM, HBM, HBM],
        out_specs=HBM,
        scratch_shapes=[
            pltpu.VMEM(half, table.dtype),
            pltpu.VMEM(half, table.dtype),
            pltpu.VMEM((shards, length - span, height), BF16),
            pltpu.VMEM((ask_rows, height), I32),
            pltpu.SMEM((ask_rows * height,), I32),
            pltpu.VMEM((8 * TILE, width), F32),
            pltpu.VMEM((8 * TILE, width), F32),
            pltpu.VMEM((shards * cap, width), BF16),
            pltpu.SemaphoreType.DMA((2,)),
            pltpu.SemaphoreType.DMA((shards,)),
            pltpu.SemaphoreType.DMA((2 * rows + 1,)),
            pltpu.SemaphoreType.DMA,
        ],
        compiler_params=pltpu.CompilerParams(vmem_limit_bytes=56 * MIB),
    )(received, table.reshape(shard_rows // TILE, TILE, width), after)


def score_kernel(span, list_hbm, replies_ref, residual_hbm, *refs):
    passages, block, width = residual_hbm.shape
    *query_refs, out_ref, wide, tile, embedded, residual_ref, list_ref, sems = refs
    listing = pltpu.make_async_copy(list_hbm, list_ref, sems.at[0])
    listing.start()
    load = pltpu.make_async_copy(residual_hbm, residual_ref, sems.at[1])
    load.start()
    groups, subs = lax.axis_size("groups"), lax.axis_size("sub")
    own_group, own_sub = lax.axis_index("groups"), lax.axis_index("sub")
    shards = query_refs[0].shape[0]
    height = list_ref.shape[0] // (passages + 8)
    pair = 2 if shards % 2 == 0 else 1
    ahead = 4 if shards % (4 * pair) == 0 else 1

    @pl.loop(0, replies_ref.shape[0] // 256)
    def _(i):
        at = pl.multiple_of(i * 256, 256)
        wide[pl.ds(at, 256)] = replies_ref[pl.ds(at, 256)].astype(F32)

    listing.wait()

    @pl.loop(0, passages, unroll=4)
    def _(p):
        count = list_ref[passages * height + p]

        def move(at, rows):
            for u in range(rows):
                place = list_ref[p * height + at + u]
                tile[pl.ds(p * block + at + u, 1)] = wide[pl.ds(place, 1)]

        move(0, 32)

        @pl.loop(2, (count + UNROLL - 1) // UNROLL)
        def _(i):
            move(pl.multiple_of(i * UNROLL, UNROLL), UNROLL)

    load.wait()
    line = lax.broadcasted_iota(I32, (block, width), 0)
    here = lax.broadcasted_iota(I32, (passages, pair * span), 0)
    counts = jnp.zeros((passages, pair * span), I32)
    for p in range(0, passages, 2):
        both = []
        for q in (p, p + 1):
            count = list_ref[passages * height + q]
            counts = jnp.where(here == q, count, counts)
            rows = tile[q * block : (q + 1) * block] + residual_ref[q]
            both.append(jnp.where(line < count, rows, rows[0:1]))
        embedded[p * block : (p + 2) * block] = jnp.concatenate(both, axis=0).astype(BF16)

    for step, query_ref in enumerate(query_refs):
        group = lax.rem(own_group + groups - step // subs, groups)
        sub = lax.rem(own_sub + subs - step % subs, subs)

        def columns(c):
            queries = jnp.concatenate(
                [query_ref[c * pair + e, :span] for e in range(pair)], axis=0
            )
            scores = dot_nt(embedded[...], queries)
            best = jnp.max(scores.reshape(passages, block, pair * span), axis=1)
            best = jnp.where(counts > 0, best, -3e38)
            for e in range(pair):
                device = (group * shards + c * pair + e) * subs + sub
                out_ref[device] = best[:, e * span : (e + 1) * span]

        if shards == pair * ahead:
            for c in range(ahead):
                columns(c)
        else:

            @pl.loop(0, shards // (pair * ahead))
            def _(i):
                for h in range(ahead):
                    columns(i * ahead + h)


def score(lists, replies, residuals, queries, span):
    passages, block, width = residuals.shape
    devices = len(queries) * queries[0].shape[0]
    return pl.pallas_call(
        functools.partial(score_kernel, span),
        out_shape=jax.ShapeDtypeStruct((devices, passages, span), F32),
        in_specs=[HBM, VMEM, HBM] + [VMEM] * len(queries),
        out_specs=VMEM,
        scratch_shapes=[
            pltpu.VMEM((replies.shape[0], width), F32),
            pltpu.VMEM((passages * block + UNROLL, width), F32),
            pltpu.VMEM((passages * block, width), BF16),
            pltpu.VMEM((passages, block, width), F32),
            pltpu.SMEM(lists.shape, I32),
            pltpu.SemaphoreType.DMA((2,)),
        ],
        compiler_params=pltpu.CompilerParams(vmem_limit_bytes=24 * MIB),
    )(lists, replies, residuals, *queries)


def pick_kernel(tokens, slots_ref, best_ref, out_ref):
    owned, listed = slots_ref.shape
    parts, slots_total, span = best_ref.shape
    slot = lax.broadcasted_iota(I32, (slots_total, listed), 0)
    sums = best_ref[0]
    for g in range(1, parts):
        sums = jnp.maximum(sums, best_ref[g])
    shift = tokens // 2
    while shift:
        sums = sums + pltpu.roll(sums, span - shift, 1)
        shift //= 2
    for q in range(owned):
        column = jnp.broadcast_to(sums[:, q * tokens : q * tokens + 1], (slots_total, listed))
        chosen = jnp.where(slot == slots_ref[q : q + 1], column, 0.0)
        out_ref[q : q + 1] = jnp.sum(chosen, axis=0, keepdims=True)


def pick(slots, best, tokens):
    return pl.pallas_call(
        functools.partial(pick_kernel, tokens),
        out_shape=jax.ShapeDtypeStruct(slots.shape, F32),
        compiler_params=pltpu.CompilerParams(vmem_limit_bytes=16 * MIB),
    )(slots, best)


def turned(array, axis, shift):
    size = lax.axis_size(axis)
    return lax.ppermute(array, axis, [(i, (i + shift) % size) for i in range(size)])


def body(queries, candidates, location, lengths, centroid_ids, residual_codes, centroids, buckets):
    token_count = centroid_ids.shape[0]
    passages = lengths.shape[0]
    height = token_count // passages
    width = residual_codes.shape[1]
    shard_rows = centroids.shape[0]
    shards, subs, parts = lax.axis_size("blk"), lax.axis_size("sub"), lax.axis_size("groups")
    cap = 2 * token_count // shards // parts
    owned, tokens = queries.shape[0], queries.shape[1]
    span = owned * tokens

    sent, pos = plan(
        lengths,
        centroid_ids.reshape(passages, height),
        queries.reshape(span, width),
        shards,
        shard_rows,
        cap,
        parts,
    )
    near = lax.all_to_all(sent, "blk", split_axis=0, concat_axis=0, tiled=True)
    lists, residuals, slots = prepare(
        pos,
        residual_codes.reshape(passages, height, width),
        buckets,
        location.reshape(location.shape[0] // 128, 128),
        candidates,
        block_rows(height, shards, parts),
    )
    found = fetch(near, centroids, slots, span, cap)
    replies = lax.all_to_all(
        found.reshape(shards, cap, width), "blk", split_axis=0, concat_axis=0, tiled=True
    )
    across = [near] + [turned(near, "groups", g) for g in range(1, parts)]
    spread = []
    for array in across:
        others = [turned(array, "sub", s) for s in range(1, subs)]
        own = turned(others[-1], "sub", 1) if array is near and others else array
        spread += [own] + others
    best = score(lists.reshape(lists.size), replies.reshape(shards * cap, width), residuals, spread, span)
    mine = lax.all_to_all(best, ("groups", "blk", "sub"), split_axis=0, concat_axis=0, tiled=True)
    return pick(slots, mine.reshape(parts, shards * subs * passages, span), tokens)


def solution(mesh):
    in_specs = (
        P(("groups", "blk", "sub"), None, None),
        P(("groups", "blk", "sub"), None),
        P(),
        P(("blk", "sub")),
        P(("blk", "sub")),
        P(("blk", "sub"), None),
        P("blk", None),
        P(),
    )
    out_specs = P(("groups", "blk", "sub"), None)
    return jax.shard_map(body, mesh=mesh, in_specs=in_specs, out_specs=out_specs, check_vma=False)
```
